128 devices in a mesh: gx: 8 (over x, core), gy: 16 (over z, y).
Axes of the slice: x: 4, y: 4, z: 4, core: 2. Of those that a mesh axis runs over, the one named last changes fastest.
Arguments:
- feats: bfloat16 [64, 524288], P(None, ('gx', 'gy')), may hold values from -6 to 6
- face_rows: int32 [128, 4, 128], P(('gx', 'gy')), may hold values from 0 to 4095
- neighbours: int32 [27, 524288], P(None, ('gx', 'gy')), may hold values from -1 to 4607, as said below
- z_dest: int32 [2, 524288], P(None, ('gx', 'gy')), may hold values from 0 to 4095, as said below
- h_dest: int32 [2, 524288], P(None, ('gx', 'gy')), may hold values from 0 to 4095, as said below
- conv_weight: bfloat16 [27, 64, 64], replicated, may hold values from -0.15625 to 0.15625
- qkv_weight: bfloat16 [2, 64, 192], replicated, may hold values from -4 to 4
- out_weight: bfloat16 [2, 64, 64], replicated, may hold values from -0.75 to 0.75
- up_weight: bfloat16 [2, 64, 256], replicated, may hold values from -0.75 to 0.75
- down_weight: bfloat16 [2, 256, 64], replicated, may hold values from -0.375 to 0.375
- norm_gains: float32 [5, 64], replicated, may hold values from 0.1 to 1.9
Outputs:
- result: bfloat16 [64, 524288], P(None, ('gx', 'gy'))
The draws below stay inside these ranges and needn't reach their ends.
Inputs may be any that keep to these rules, and one draw needn't show every extreme that they name: `neighbours`: entry 13 of each point is the point itself; other entries are -1 (no neighbour), a local point 0 to 4095, or 4096 + f * 128 + r for row r of the f-th block of face points in extended. `z_dest`: row 0 is the owner device, row 1 the slot in the owner's patch buffer; all (owner, slot) pairs are distinct, so every device owns 4096 points. The points of one device go 48 to each of half of the devices and a third of 48 to each of the other half. `h_dest`: same form and counts as z_dest, for the Hilbert order. `face_rows`: rows 0 to 3 list points of the tile's lower x, upper x, lower y and upper y faces.
All inputs are finite; a program needn't handle non-finite values.
Results may differ from the reference program's by a relative error of at most 0.019.
The reference program's roundings to bfloat16 on the way count: a program that leaves them out, or rounds other values in their place, can miss the bound.
Values may be sent and summed in bfloat16 or wider, within the bound.
No kernel may reach another device: no remote copies, remote signals or barrier semaphores. Data moves between devices by JAX's collectives and lax.ppermute only.
A program may use at most 128 MiB of HBM per device.

```python
import jax
import jax.numpy as jnp
from jax import lax

C = 64
HEADS = 4
HEAD_DIM = 16
HID = 256
PATCH = 1024
OFFSETS = 27
P_DEV = 4096
FACE = 128
CAP = 48
POINTS = 524288
N_GX = 8
N_GY = 16
DEVICES = 128


def serial_positions(key):
    devices = POINTS // P_DEV
    half_count = devices // 2
    lighter = CAP // 3
    key_parts = jax.random.split(key, 5)
    row_perm = jax.random.permutation(key_parts[0], devices)
    col_perm = jax.random.permutation(key_parts[1], devices)
    shifts = jax.random.permutation(key_parts[2], devices)
    column = jnp.arange(P_DEV, dtype=jnp.int32)
    local_scores = jax.random.randint(key_parts[3], (devices, P_DEV), 0, 4096) * P_DEV + column[None, :]
    ordering = jnp.argsort(local_scores, axis=1)
    groups = jnp.where(column < half_count * CAP, column // CAP, half_count + (column - half_count * CAP) // lighter)
    owners = row_perm[(col_perm[:, None] + shifts[groups][None, :]) % devices]
    slot_scores = jax.random.randint(key_parts[4], (devices, P_DEV), 0, 4096) * P_DEV + column[None, :]
    slot_table = jnp.argsort(slot_scores, axis=1).astype(jnp.int32)
    slots = slot_table[owners, column[None, :]]
    sources = jnp.arange(devices, dtype=jnp.int32)[:, None]
    owner_out = jnp.zeros((devices, P_DEV), jnp.int32).at[sources, ordering].set(owners.astype(jnp.int32))
    slot_out = jnp.zeros((devices, P_DEV), jnp.int32).at[sources, ordering].set(slots)
    return jnp.stack([owner_out.reshape(-1), slot_out.reshape(-1)])


def draw_z_dest(key, part):
    key = jax.random.fold_in(key, 11)
    return serial_positions(key)


def draw_h_dest(key, part):
    key = jax.random.fold_in(key, 12)
    return serial_positions(key)


def draw_neighbours(key, part):
    key = jax.random.fold_in(key, 21)
    devices = POINTS // P_DEV
    key_parts = jax.random.split(key, 3)
    local_rows = jax.random.randint(key_parts[0], (OFFSETS, devices, P_DEV), 0, P_DEV)
    remote = P_DEV + jax.random.randint(key_parts[1], (OFFSETS, devices, P_DEV), 0, 4 * FACE)
    chooser = jax.random.randint(key_parts[2], (OFFSETS, devices, P_DEV), 0, 8)
    picked = jnp.where(chooser == 0, remote, jnp.where(chooser < 3, -1, local_rows))
    column = jnp.arange(P_DEV, dtype=jnp.int32)
    picked = picked.at[OFFSETS // 2].set(jnp.broadcast_to(column, (devices, P_DEV)))
    forced = jnp.where(column < 4 * FACE, P_DEV + column, jnp.where(column == 4 * FACE, -1, picked[0]))
    picked = picked.at[0].set(forced)
    return picked.reshape(OFFSETS, devices * P_DEV).astype(jnp.int32)


def draw_qkv_weight(key, part):
    key = jax.random.fold_in(key, 31)
    key_parts = jax.random.split(key, 1)
    scale = (3.0 / C) ** 0.5
    drawn = jax.random.normal(key_parts[0], (2, C, 3 * C), jnp.float32) * scale
    return jnp.clip(drawn, -4.0, 4.0).astype(jnp.bfloat16)


def touch_ends(entries, own_key, smallest, largest):
    dims = entries.shape
    index_at = [jax.random.randint(jax.random.fold_in(own_key, axis), (), 0, dims[axis]) for axis in range(len(dims))]
    entries = entries.at[tuple(index_at)].set(smallest)
    longest = dims.index(max(dims))
    index_at[longest] = (index_at[longest] + 1) % dims[longest]
    return entries.at[tuple(index_at)].set(largest)


def block_scale(key, dims, cuts, low, largest):
    factor_of, own = 1.0, jax.random.fold_in(key, 6)
    for dim, shards_of in cuts:
        heights = jnp.exp(jax.random.uniform(jax.random.fold_in(own, dim), (shards_of,), jnp.float32, low / len(cuts), largest / len(cuts)))
        factor_of = factor_of * jnp.repeat(heights, dims[dim] // shards_of).reshape([-1 if axis == dim else 1 for axis in range(len(dims))])
    return factor_of


def bell_draw(rng, shape, scale, most, cuts=(), kind=jnp.bfloat16):
    values = jax.random.normal(rng, shape, jnp.float32) * scale
    if len(cuts) > 0:
        values = block_scale(rng, shape, cuts, -0.22, 0.18) * values
    return jnp.clip(values, min=-most, max=most).astype(kind)


def setup_inputs(seed: int = 0) -> dict:
    keys = jax.random.split(jax.random.key(seed), 12)
    return {
        "feats": bell_draw(keys[0], (C, POINTS), 1.0, 6.0, ((1, 128),)),
        "face_rows": touch_ends(jax.random.randint(keys[1], (DEVICES, 4, FACE), 0, P_DEV), jax.random.fold_in(keys[1], 1), 0, P_DEV - 1).astype(jnp.int32),
        "neighbours": draw_neighbours(jax.random.fold_in(keys[11], 71), 0),
        "z_dest": draw_z_dest(jax.random.fold_in(keys[11], 71), 0),
        "h_dest": draw_h_dest(jax.random.fold_in(keys[11], 71), 0),
        "conv_weight": bell_draw(keys[5], (OFFSETS, C, C), (OFFSETS * C) ** -0.5, 0.15625),
        "qkv_weight": draw_qkv_weight(jax.random.fold_in(keys[11], 71), 0),
        "out_weight": bell_draw(keys[7], (2, C, C), C ** -0.5, 0.75),
        "up_weight": bell_draw(keys[8], (2, C, HID), C ** -0.5, 0.75),
        "down_weight": bell_draw(keys[9], (2, HID, C), HID ** -0.5, 0.375),
        "norm_gains": jnp.clip(1.0 + 0.18 * jax.random.normal(keys[10], (5, C), jnp.float32), 0.1, 1.9),
    }


EPS = 1e-05

def layer_norm(values, scale_gain):
    average = lax.optimization_barrier(jnp.mean(values, axis=0, keepdims=True))
    centred = values - average
    spread = lax.optimization_barrier(jnp.mean(centred * centred, axis=0, keepdims=True))
    return centred * lax.rsqrt(spread + EPS) * scale_gain[:, None]

def positional(extended, offsets_idx, conv_weight, scale_gain, own_cols):
    last_col = extended.shape[1] - 1
    resolved = jnp.where(offsets_idx < 0, last_col, offsets_idx)

    def accumulate(running, offset_pair):
        kernel, columns = offset_pair
        gathered = jnp.take(extended, columns, axis=0 + 1).astype(jnp.float32)
        return (running + jnp.dot(kernel.astype(jnp.float32).T, gathered, preferred_element_type=jnp.float32), None)
    blank = jnp.zeros(own_cols.shape, jnp.float32)
    convolved, _ = lax.scan(accumulate, blank, (conv_weight, resolved))
    return (own_cols.astype(jnp.float32) + layer_norm(convolved, scale_gain)).astype(jnp.bfloat16)

def patch_block(patch_cols, qkv_w, out_w, up_w, down_w, gain_a, gain_b):
    channels, length = patch_cols.shape
    based = patch_cols.astype(jnp.float32)
    normed = layer_norm(based, gain_a).astype(jnp.bfloat16)
    qkv = jnp.dot(qkv_w.T, normed, preferred_element_type=jnp.float32).astype(jnp.bfloat16)
    split_qkv = qkv.reshape(3, HEADS, HEAD_DIM, length).astype(jnp.float32)
    scores = jnp.einsum('hdq,hdk->hqk', split_qkv[0], split_qkv[1]) * HEAD_DIM ** (-0.5)
    row_max = lax.optimization_barrier(jnp.max(scores, axis=2, keepdims=True))
    weights = jnp.exp(scores - row_max)
    probabilities = (weights / lax.optimization_barrier(jnp.sum(weights, axis=2, keepdims=True))).astype(jnp.bfloat16)
    mixed_out = jnp.einsum('hqk,hdk->hdq', probabilities.astype(jnp.float32), split_qkv[2])
    mixed_out = mixed_out.astype(jnp.bfloat16).reshape(channels, length)
    residual = based + jnp.dot(out_w.T, mixed_out, preferred_element_type=jnp.float32)
    normed_b = layer_norm(residual, gain_b).astype(jnp.bfloat16)
    hidden = jax.nn.gelu(jnp.dot(up_w.T, normed_b, preferred_element_type=jnp.float32), approximate=False)
    hidden = hidden.astype(jnp.bfloat16)
    return (residual + jnp.dot(down_w.T, hidden, preferred_element_type=jnp.float32)).astype(jnp.bfloat16)

def serial_block(layout, qkv_w, out_w, up_w, down_w, gain_a, gain_b):
    patches = layout.shape[1] // PATCH

    def advance(patch_index, outcome):
        offset_col = (patch_index * PATCH).astype(jnp.int32)
        patch_cols = lax.dynamic_slice_in_dim(layout, offset_col, PATCH, 1)
        done = patch_block(patch_cols, qkv_w, out_w, up_w, down_w, gain_a, gain_b)
        return lax.dynamic_update_slice_in_dim(outcome, done, offset_col, 1)
    return lax.fori_loop(0, patches, advance, jnp.zeros_like(layout))

def reference(feats, face_rows, neighbours, z_dest, h_dest, conv_weight, qkv_weight, out_weight, up_weight, down_weight, norm_gains):
    devices = N_GX * N_GY
    channels = feats.shape[0]
    tiles = jnp.transpose(feats.reshape(channels, N_GX, N_GY, P_DEV), (1, 2, 0, 3))
    face_list = face_rows.reshape(N_GX, N_GY, 4, FACE)
    faces = jax.vmap(jax.vmap(lambda tile_cols, listed: jnp.take(tile_cols, listed, axis=1)))(tiles, face_list)
    empty_x = jnp.zeros((1, N_GY, channels, FACE), feats.dtype)
    lower_x = jnp.concatenate([empty_x, faces[:-1, :, :, 1]], axis=0)
    upper_x = jnp.concatenate([faces[1:, :, :, 0], empty_x], axis=0)
    empty_y = jnp.zeros((N_GX, 1, channels, FACE), feats.dtype)
    lower_y = jnp.concatenate([empty_y, faces[:, :-1, :, 3]], axis=1)
    upper_y = jnp.concatenate([faces[:, 1:, :, 2], empty_y], axis=1)
    closing = jnp.zeros((N_GX, N_GY, channels, 1), feats.dtype)
    extended = jnp.concatenate([tiles, lower_x, upper_x, lower_y, upper_y, closing], axis=3)
    extended = extended.reshape(devices, channels, P_DEV + 4 * FACE + 1)
    offsets_first = jnp.transpose(neighbours.reshape(OFFSETS, devices, P_DEV), (1, 0, 2))
    own_cols = tiles.reshape(devices, channels, P_DEV)
    encoded = lax.map(lambda bundle: positional(bundle[0], bundle[1], conv_weight, norm_gains[0], bundle[2]), (extended, offsets_first, own_cols))
    encoded = jnp.transpose(encoded, (1, 0, 2)).reshape(channels, devices * P_DEV)
    z_place = (z_dest[0] * P_DEV + z_dest[1]).astype(jnp.int32)
    zorder = jnp.zeros_like(encoded).at[:, z_place].set(encoded)
    first_out = serial_block(zorder, qkv_weight[0], out_weight[0], up_weight[0], down_weight[0], norm_gains[1], norm_gains[2])
    home = jnp.take(first_out, z_place, axis=1)
    h_place = (h_dest[0] * P_DEV + h_dest[1]).astype(jnp.int32)
    hilbert = jnp.zeros_like(home).at[:, h_place].set(home)
    return serial_block(hilbert, qkv_weight[1], out_weight[1], up_weight[1], down_weight[1], norm_gains[3], norm_gains[4])
```

```python
import functools

import jax
import jax.numpy as jnp
from jax import lax
from jax.experimental import pallas as pl
from jax.experimental.pallas import tpu as pltpu
from jax.sharding import PartitionSpec as P

HEADS = 4
HEAD_DIM = 16
PATCH = 1024
C = 64
PTS = 4096
FACE = 128
EXT = PTS + 4 * FACE
TROWS = EXT + 8
DEV = 128
CAP = 48
HALF = CAP // 2
PACK = DEV * HALF
PAIRS = 13
BLK = 512
UN = 8
EPS = 1e-05
VMEM = 60 * 2**20
BF = jnp.bfloat16
F32 = jnp.float32


def lane_norm(values, gain):
    average = jnp.mean(values, axis=1, keepdims=True)
    centred = values - average
    spread = jnp.mean(centred * centred, axis=1, keepdims=True)
    return centred * lax.rsqrt(spread + EPS) * gain


def chan_norm(values, gain):
    average = jnp.mean(values, axis=0, keepdims=True)
    centred = values - average
    spread = jnp.mean(centred * centred, axis=0, keepdims=True)
    return centred * lax.rsqrt(spread + EPS) * gain


def low_lanes(rows):
    return lax.broadcasted_iota(jnp.int32, (rows, 128), 1) < C


def pack_rows(rows_ref, out_ref):
    def part(b, _):
        at = pl.multiple_of(b * 512, 512)
        low = rows_ref[pl.ds(at, 512), :]
        high = pltpu.roll(rows_ref[pl.ds(at + PACK, 512), :], C, 1)
        out_ref[pl.ds(at, 512), :] = jnp.where(low_lanes(512), low, high).astype(BF)
        return 0

    lax.fori_loop(0, PACK // 512, part, 0)


def unpack_rows(in_ref, rows_ref):
    def part(b, _):
        at = pl.multiple_of(b * 512, 512)
        both = in_ref[pl.ds(at, 512), :].astype(F32)
        rows_ref[pl.ds(at, 512), :] = both
        rows_ref[pl.ds(at + PACK, 512), :] = pltpu.roll(both, C, 1)
        return 0

    lax.fori_loop(0, PACK // 512, part, 0)


def conv_kernel(idx_ref, place_ref, ext_ref, pair_ref, self_ref, gain_ref, out_ref, table, sums, rows):
    step = pl.program_id(0)

    @pl.when(step == 0)
    def _():
        def fill(b, _):
            at = pl.multiple_of(b * 512, 512)
            chunk = ext_ref[pl.ds(at, 512), :]
            for j in range(PAIRS):
                table[pl.ds(pl.multiple_of(j * TROWS + at, 8), 512), :] = jnp.dot(
                    chunk, pair_ref[j], preferred_element_type=F32
                )
            return 0

        lax.fori_loop(0, EXT // 512, fill, 0)
        for j in range(PAIRS):
            table[j * TROWS + EXT : (j + 1) * TROWS, :] = jnp.zeros((TROWS - EXT, 128), F32)

    low_row = low_lanes(1)

    def gather(g, _):
        for u in range(UN):
            i = g * UN + u
            even, odd = None, None
            for j in range(PAIRS):
                a = table[pl.ds(idx_ref[2 * j, i], 1), :]
                b = table[pl.ds(idx_ref[2 * j + 1, i], 1), :]
                even = a if even is None else even + a
                odd = b if odd is None else odd + b
            sums[pl.ds(i, 1), :] = jnp.where(low_row, even, odd)
        return 0

    lax.fori_loop(0, BLK // UN, gather, 0)
    own = ext_ref[pl.ds(pl.multiple_of(step * BLK, BLK), BLK), :]
    both = sums[...]
    conv = both[:, :C] + both[:, C:] + jnp.dot(own, self_ref[...], preferred_element_type=F32)
    encoded = own.astype(F32) + lane_norm(conv, gain_ref[...])
    sums[:, :C] = encoded

    def scatter(g, _):
        for u in range(UN):
            i = g * UN + u
            rows[pl.ds(place_ref[step * BLK + i], 1), :] = sums[pl.ds(i, 1), :]
        return 0

    lax.fori_loop(0, BLK // UN, scatter, 0)

    @pl.when(step == pl.num_programs(0) - 1)
    def _():
        pack_rows(rows, out_ref)


def conv_send(idx, place, ext_rows, pair_w, self_w, gain):
    steps = PTS // BLK
    return pl.pallas_call(
        conv_kernel,
        grid=(steps,),
        in_specs=[
            pl.BlockSpec((2 * PAIRS, BLK), lambda s: (0, s), memory_space=pltpu.SMEM),
            pl.BlockSpec(memory_space=pltpu.SMEM),
            pl.BlockSpec((EXT, C), lambda s: (0, 0)),
            pl.BlockSpec((PAIRS, C, 128), lambda s: (0, 0, 0)),
            pl.BlockSpec((C, C), lambda s: (0, 0)),
            pl.BlockSpec((1, C), lambda s: (0, 0)),
        ],
        out_specs=pl.BlockSpec((PACK, 128), lambda s: (0, 0)),
        out_shape=jax.ShapeDtypeStruct((PACK, 128), BF),
        scratch_shapes=[
            pltpu.VMEM((PAIRS * TROWS, 128), F32),
            pltpu.VMEM((BLK, 128), F32),
            pltpu.VMEM((2 * PACK, 128), F32),
        ],
        compiler_params=pltpu.CompilerParams(vmem_limit_bytes=VMEM),
        cost_estimate=pl.CostEstimate(flops=10**11, bytes_accessed=10**6, transcendentals=0),
        name="conv_send",
    )(idx, place, ext_rows, pair_w, self_w, gain)


def relay_kernel(from_ref, to_ref, in_ref, out_ref, source, target):
    unpack_rows(in_ref, source)

    def move(g, _):
        for u in range(UN):
            i = g * UN + u
            target[pl.ds(to_ref[i], 1), :] = source[pl.ds(from_ref[i], 1), :]
        return 0

    lax.fori_loop(0, PTS // UN, move, 0)
    pack_rows(target, out_ref)


def relay(place_from, place_to, packed):
    return pl.pallas_call(
        relay_kernel,
        in_specs=[
            pl.BlockSpec(memory_space=pltpu.SMEM),
            pl.BlockSpec(memory_space=pltpu.SMEM),
            pl.BlockSpec(memory_space=pltpu.VMEM),
        ],
        out_specs=pl.BlockSpec(memory_space=pltpu.VMEM),
        out_shape=jax.ShapeDtypeStruct((PACK, 128), BF),
        scratch_shapes=[
            pltpu.VMEM((2 * PACK, 128), F32),
            pltpu.VMEM((2 * PACK, 128), F32),
        ],
        compiler_params=pltpu.CompilerParams(vmem_limit_bytes=VMEM),
        cost_estimate=pl.CostEstimate(flops=10**9, bytes_accessed=10**6, transcendentals=0),
        name="relay",
    )(place_from, place_to, packed)


def patch_math(x, qkv_ref, outw_ref, up_ref, down_ref, gain_a_ref, gain_b_ref, mixed):
    normed = chan_norm(x, gain_a_ref[...]).astype(BF)
    qkv = jnp.dot(qkv_ref[...], normed, preferred_element_type=F32).astype(BF)
    queries = qkv[:C].astype(F32) * HEAD_DIM**-0.5
    keys = qkv[C : 2 * C].astype(F32).T.astype(BF)
    head_of = lax.broadcasted_iota(jnp.int32, (C, PATCH), 0) // HEAD_DIM
    ones = jnp.ones((HEAD_DIM, PATCH), BF)
    for h in range(HEADS):
        masked = jnp.where(head_of == h, queries, 0.0).astype(BF)
        scores = jnp.dot(keys, masked, preferred_element_type=F32)
        weights = jnp.exp(scores - jnp.max(scores, axis=0, keepdims=True)).astype(BF)
        first = 2 * C + h * HEAD_DIM
        values = jnp.concatenate([qkv[first : first + HEAD_DIM], ones], axis=0)
        summed = jnp.dot(values, weights, preferred_element_type=F32)
        mixed[h * HEAD_DIM : (h + 1) * HEAD_DIM, :] = (
            summed[:HEAD_DIM] / summed[HEAD_DIM : HEAD_DIM + 1]
        ).astype(BF)
    residual = x + jnp.dot(outw_ref[...], mixed[...], preferred_element_type=F32)
    normed_b = chan_norm(residual, gain_b_ref[...]).astype(BF)
    raised = jnp.dot(up_ref[...], normed_b, preferred_element_type=F32)
    hidden = (0.5 * raised * (1.0 + lax.erf(raised * 0.5**0.5))).astype(BF)
    return residual + jnp.dot(down_ref[...], hidden, preferred_element_type=F32)


def block_kernel(
    back, slot_ref, in_ref, qkv_ref, outw_ref, up_ref, down_ref, ga_ref, gb_ref, out_ref,
    source, rows, mixed,
):
    unpack_rows(in_ref, source)

    def place(g, _):
        for u in range(UN):
            i = g * UN + u
            rows[pl.ds(slot_ref[i], 1), :] = source[pl.ds(i, 1), :]
        return 0

    lax.fori_loop(0, 2 * PACK // UN, place, 0)

    def patch(p, _):
        at = pl.multiple_of(p * PATCH, PATCH)
        x = rows[pl.ds(at, PATCH), :].T[:C]
        y = patch_math(x, qkv_ref, outw_ref, up_ref, down_ref, ga_ref, gb_ref, mixed)
        if back:
            rows[pl.ds(at, PATCH), :] = jnp.concatenate([y, y], axis=0).T
        else:
            out_ref[:, pl.ds(at, PATCH)] = y.astype(BF)
        return 0

    lax.fori_loop(0, PTS // PATCH, patch, 0)
    if back:
        low_row = low_lanes(1)

        def fetch(g, _):
            for u in range(UN):
                i = g * UN + u
                low = rows[pl.ds(slot_ref[i], 1), :]
                high = rows[pl.ds(slot_ref[i + PACK], 1), :]
                source[pl.ds(i, 1), :] = jnp.where(low_row, low, high)
            return 0

        lax.fori_loop(0, PACK // UN, fetch, 0)
        out_ref[...] = source[0:PACK, :].astype(BF)


def block(back, slots, packed, qkv_w, out_w, up_w, down_w, gain_a, gain_b):
    out = (PACK, 128) if back else (C, PTS)
    return pl.pallas_call(
        functools.partial(block_kernel, back),
        in_specs=[pl.BlockSpec(memory_space=pltpu.SMEM)]
        + [pl.BlockSpec(memory_space=pltpu.VMEM)] * 7,
        out_specs=pl.BlockSpec(memory_space=pltpu.VMEM),
        out_shape=jax.ShapeDtypeStruct(out, BF),
        scratch_shapes=[
            pltpu.VMEM((2 * PACK, 128), F32),
            pltpu.VMEM((PTS + 8, 128), F32),
            pltpu.VMEM((C, PATCH), BF),
        ],
        compiler_params=pltpu.CompilerParams(vmem_limit_bytes=VMEM),
        cost_estimate=pl.CostEstimate(flops=4 * 10**10, bytes_accessed=10**6, transcendentals=0),
        name="block_back" if back else "block_last",
    )(slots, packed, qkv_w.T, out_w.T, up_w.T, down_w.T, gain_a[:, None], gain_b[:, None])


def beside(block_cols, sides, width):
    for axis, dim in sides:
        count = lax.axis_size(axis)
        forward = [(i, i + 1) for i in range(count - 1)]
        backward = [(target, source) for source, target in forward]
        low = lax.ppermute(block_cols[:, 1], axis, forward)
        high = lax.ppermute(block_cols[:, 0], axis, backward)
    return low, high


def places(dest):
    owners, slots = dest[0], dest[1]
    lanes = 128
    matches = (owners[None, :] == jnp.arange(DEV, dtype=jnp.int32)[:, None]).astype(BF)
    grouped = matches.reshape(DEV, PTS // lanes, lanes)
    index_row = jnp.arange(lanes, dtype=jnp.int32)
    strict = (index_row[:, None] < index_row[None, :]).astype(BF)
    within = jnp.einsum("dbi,ij->dbj", grouped, strict, preferred_element_type=F32)
    totals = jnp.sum(grouped.astype(F32), axis=2)
    before = jnp.cumsum(totals, axis=1) - totals
    ranking = jnp.sum(grouped.astype(F32) * (within + before[:, :, None]), axis=0)
    ranking = ranking.reshape(PTS).astype(jnp.int32)
    place = (ranking // HALF) * PACK + owners * HALF + ranking % HALF
    ranks = (ranking[:, None] == jnp.arange(CAP, dtype=jnp.int32)[None, :]).astype(BF)
    coded = slots + 1
    high = ranks * (coded // 64).astype(BF)[:, None]
    low = ranks * (coded % 64).astype(BF)[:, None]
    listed = jnp.dot(
        matches, jnp.concatenate([high, low], axis=1), preferred_element_type=F32
    ).astype(jnp.int32)
    listed = listed[:, :CAP] * 64 + listed[:, CAP:]
    return place, jnp.where(listed == 0, PTS, listed - 1)


def exchange(packed):
    shaped = packed.reshape(DEV, HALF, 128)
    moved = lax.all_to_all(shaped, ("gx", "gy"), split_axis=0, concat_axis=0, tiled=True)
    return moved.reshape(PACK, 128)


def local(
    feats,
    face_rows,
    neighbours,
    z_dest,
    h_dest,
    conv_weight,
    qkv_weight,
    out_weight,
    up_weight,
    down_weight,
    norm_gains,
):
    picked = jnp.take(feats, face_rows[0], axis=1)
    low_x, high_x = beside(picked[:, 0:2], (("gx", 1),), 1)
    low_y, high_y = beside(picked[:, 2:4], (("gy", 1),), 1)
    ext_rows = jnp.concatenate([feats, low_x, high_x, low_y, high_y], axis=1).T

    z_place, z_list = places(z_dest)
    h_place, h_list = places(h_dest)
    slots = lax.all_to_all(
        jnp.concatenate([z_list, h_list], axis=1), ("gx", "gy"),
        split_axis=0, concat_axis=0, tiled=True,
    )
    slots = slots.reshape(DEV, 4, HALF).transpose(1, 0, 2).reshape(2, 2 * PACK)

    others = jnp.concatenate([neighbours[:PAIRS], neighbours[PAIRS + 1 :]], axis=0)
    base = (jnp.arange(2 * PAIRS, dtype=jnp.int32) // 2 * TROWS)[:, None]
    idx = jnp.where(others < 0, EXT, others) + base
    pair_w = jnp.concatenate([conv_weight[:PAIRS], conv_weight[PAIRS + 1 :]], axis=0)
    pair_w = jnp.concatenate([pair_w[0::2], pair_w[1::2]], axis=2)

    sent = conv_send(idx, z_place, ext_rows, pair_w, conv_weight[PAIRS], norm_gains[0:1])
    returned = block(
        True, slots[0], exchange(sent), qkv_weight[0], out_weight[0], up_weight[0],
        down_weight[0], norm_gains[1], norm_gains[2],
    )
    resent = relay(z_place, h_place, exchange(returned))
    return block(
        False, slots[1], exchange(resent), qkv_weight[1], out_weight[1], up_weight[1],
        down_weight[1], norm_gains[3], norm_gains[4],
    )


def solution(mesh):
    placed = (
        P(None, ("gx", "gy")),
        P(("gx", "gy"), None, None),
        P(None, ("gx", "gy")),
        P(None, ("gx", "gy")),
        P(None, ("gx", "gy")),
        P(),
        P(),
        P(),
        P(),
        P(),
        P(),
    )
    return jax.shard_map(
        local, mesh=mesh, in_specs=placed, out_specs=P(None, ("gx", "gy")), check_vma=False
    )
```

```python
import functools

import jax
import jax.numpy as jnp
from jax import lax
from jax.experimental import pallas as pl
from jax.experimental.pallas import tpu as pltpu
from jax.sharding import PartitionSpec as P

HEADS = 4
HEAD_DIM = 16
PATCH = 1024
C = 64
PTS = 4096
FACE = 128
EXT = PTS + 4 * FACE
TROWS = EXT + 8
DEV = 128
CAP = 48
HALF = CAP // 2
PACK = DEV * HALF
PAIRS = 13
BLK = 512
UN = 16
GROUP = 32
GROUPS = PTS // GROUP
LISTS = 4
LOG2_E = 1.4426950408889634
SAFE = 72.0
EPS = 1e-05
VMEM = 60 * 2**20
BF = jnp.bfloat16
F32 = jnp.float32


def lane_norm(values, gain):
    average = jnp.mean(values, axis=1, keepdims=True)
    centred = values - average
    spread = jnp.mean(centred * centred, axis=1, keepdims=True)
    return centred * lax.rsqrt(spread + EPS) * gain


def chan_norm(values, gain):
    average = jnp.mean(values, axis=0, keepdims=True)
    centred = values - average
    spread = jnp.mean(centred * centred, axis=0, keepdims=True)
    return centred * lax.rsqrt(spread + EPS) * gain


def low_lanes(rows):
    return lax.broadcasted_iota(jnp.int32, (rows, 128), 1) < C


def pack_rows(rows_ref, out_ref):
    def part(b, _):
        at = pl.multiple_of(b * 512, 512)
        low = rows_ref[pl.ds(at, 512), :]
        high = pltpu.roll(rows_ref[pl.ds(at + PACK, 512), :], C, 1)
        out_ref[pl.ds(at, 512), :] = jnp.where(low_lanes(512), low, high).astype(BF)
        return 0

    lax.fori_loop(0, PACK // 512, part, 0)


def unpack_rows(in_ref, rows_ref):
    def part(b, _):
        at = pl.multiple_of(b * 512, 512)
        both = in_ref[pl.ds(at, 512), :].astype(F32)
        rows_ref[pl.ds(at, 512), :] = both
        rows_ref[pl.ds(at + PACK, 512), :] = pltpu.roll(both, C, 1)
        return 0

    lax.fori_loop(0, PACK // 512, part, 0)


def move_rows(count, read, place_ref, rows_ref):
    def move(g, _):
        at = g * UN
        taken = [read(at + u) for u in range(UN)]
        for u in range(UN):
            rows_ref[pl.ds(place_ref[at + u], 1), :] = taken[u]
        return 0

    lax.fori_loop(0, count // UN, move, 0)


def conv_kernel(idx_ref, place_ref, ext_ref, pair_ref, self_ref, gain_ref, out_ref, *scratch):
    table, sums, rows = scratch[:3]
    lists, sems = scratch[3 : 3 + LISTS], scratch[3 + LISTS]

    def list_copy(g, b):
        return pltpu.make_async_copy(idx_ref.at[g], lists[b], sems.at[b])

    for b in range(LISTS):
        list_copy(b, b).start()

    def fill(b, _):
        at = pl.multiple_of(b * 512, 512)
        chunk = ext_ref[pl.ds(at, 512), :]
        for j in range(PAIRS):
            table[pl.ds(pl.multiple_of(j * TROWS + at, 8), 512), :] = jnp.dot(
                chunk, pair_ref[j], preferred_element_type=F32
            )
        return 0

    lax.fori_loop(0, EXT // 512, fill, 0)
    for j in range(PAIRS):
        table[j * TROWS + EXT : (j + 1) * TROWS, :] = jnp.zeros((TROWS - EXT, 128), F32)

    low_row = low_lanes(1)

    def gather(step, _):
        for b in range(LISTS):
            g = step * LISTS + b
            list_copy(g, b).wait()
            for u in range(GROUP):
                even, odd = None, None
                for j in range(PAIRS):
                    at = 2 * j * GROUP + u
                    first = table[pl.ds(lists[b][at // 128, at % 128], 1), :]
                    at = at + GROUP
                    second = table[pl.ds(lists[b][at // 128, at % 128], 1), :]
                    even = first if even is None else even + first
                    odd = second if odd is None else odd + second
                sums[pl.ds(u * GROUPS + g, 1), :] = jnp.where(low_row, even, odd)
            list_copy(jnp.minimum(g + LISTS, GROUPS - 1), b).start()
        return 0

    lax.fori_loop(0, GROUPS // LISTS, gather, 0)
    for b in range(LISTS):
        list_copy(GROUPS - 1, b).wait()

    def finish(b, _):
        at = pl.multiple_of(b * BLK, BLK)
        own = ext_ref[pl.ds(at, BLK), :]
        both = sums[pl.ds(at, BLK), :]
        conv = both[:, :C] + both[:, C:] + jnp.dot(own, self_ref[...], preferred_element_type=F32)
        sums[pl.ds(at, BLK), :C] = own.astype(F32) + lane_norm(conv, gain_ref[...])
        return 0

    lax.fori_loop(0, PTS // BLK, finish, 0)
    move_rows(PTS, lambda i: sums[pl.ds(i, 1), :], place_ref, rows)
    pack_rows(rows, out_ref)


def conv_send(idx, place, ext_rows, pair_w, self_w, gain):
    return pl.pallas_call(
        conv_kernel,
        in_specs=[pl.BlockSpec(memory_space=pl.ANY), pl.BlockSpec(memory_space=pltpu.SMEM)]
        + [pl.BlockSpec(memory_space=pltpu.VMEM)] * 4,
        out_specs=pl.BlockSpec(memory_space=pltpu.VMEM),
        out_shape=jax.ShapeDtypeStruct((PACK, 128), BF),
        scratch_shapes=[
            pltpu.VMEM((PAIRS * TROWS, 128), F32),
            pltpu.VMEM((PTS, 128), F32),
            pltpu.VMEM((2 * PACK, 128), F32),
        ]
        + [pltpu.SMEM((8, 128), jnp.int32)] * LISTS
        + [pltpu.SemaphoreType.DMA((LISTS,))],
        compiler_params=pltpu.CompilerParams(vmem_limit_bytes=VMEM),
        cost_estimate=pl.CostEstimate(flops=10**11, bytes_accessed=10**6, transcendentals=0),
        name="conv_send",
    )(idx, place, ext_rows, pair_w, self_w, gain)


def relay_kernel(from_ref, to_ref, in_ref, out_ref, source, target):
    unpack_rows(in_ref, source)

    move_rows(PTS, lambda i: source[pl.ds(from_ref[i], 1), :], to_ref, target)
    pack_rows(target, out_ref)


def relay(place_from, place_to, packed):
    return pl.pallas_call(
        relay_kernel,
        in_specs=[
            pl.BlockSpec(memory_space=pltpu.SMEM),
            pl.BlockSpec(memory_space=pltpu.SMEM),
            pl.BlockSpec(memory_space=pltpu.VMEM),
        ],
        out_specs=pl.BlockSpec(memory_space=pltpu.VMEM),
        out_shape=jax.ShapeDtypeStruct((PACK, 128), BF),
        scratch_shapes=[
            pltpu.VMEM((2 * PACK, 128), F32),
            pltpu.VMEM((2 * PACK, 128), F32),
        ],
        compiler_params=pltpu.CompilerParams(vmem_limit_bytes=VMEM),
        cost_estimate=pl.CostEstimate(flops=10**9, bytes_accessed=10**6, transcendentals=0),
        name="relay",
    )(place_from, place_to, packed)


def patch_math(x, qkv_ref, outw_ref, up_ref, down_ref, gain_a_ref, gain_b_ref, mixed):
    normed = chan_norm(x, gain_a_ref[...]).astype(BF)
    qkv = jnp.dot(qkv_ref[...], normed, preferred_element_type=F32).astype(BF)
    queries = qkv[:C].astype(F32)
    keys = qkv[C : 2 * C].astype(F32)
    keys_t = keys.T
    head_of = lax.broadcasted_iota(jnp.int32, (C, PATCH), 0) // HEAD_DIM
    ones = jnp.ones((HEAD_DIM, PATCH), BF)

    def of_head(h, values):
        return jnp.where(head_of == h, values, 0.0)

    def mix(h, weights):
        first = 2 * C + h * HEAD_DIM
        values = jnp.concatenate([qkv[first : first + HEAD_DIM], ones], axis=0)
        summed = jnp.dot(values, weights, preferred_element_type=F32)
        mixed[h * HEAD_DIM : (h + 1) * HEAD_DIM, :] = (
            summed[:HEAD_DIM] / summed[HEAD_DIM : HEAD_DIM + 1]
        ).astype(BF)

    def longest(values):
        squares = (values * values).reshape(HEADS, HEAD_DIM, PATCH)
        return jnp.max(jnp.sum(squares, axis=1), axis=1, keepdims=True)

    reach = jnp.max(longest(queries) * longest(keys))
    safe = reach <= (SAFE * HEAD_DIM**0.5) ** 2

    @pl.when(safe)
    def _():
        scaled = queries * (HEAD_DIM**-0.5 * LOG2_E)
        upper = scaled.astype(BF).astype(F32)
        lower = scaled - upper
        keys_2 = jnp.concatenate([keys_t, keys_t], axis=1).astype(BF)
        for h in range(HEADS):
            split = jnp.concatenate([of_head(h, upper), of_head(h, lower)], axis=0).astype(BF)
            scores = jnp.dot(keys_2, split, preferred_element_type=F32)
            mix(h, jnp.exp2(scores).astype(BF))

    @pl.when(jnp.logical_not(safe))
    def _():
        keys_1 = keys_t.astype(BF)
        for h in range(HEADS):
            one_head = of_head(h, queries * HEAD_DIM**-0.5).astype(BF)
            scores = jnp.dot(keys_1, one_head, preferred_element_type=F32)
            mix(h, jnp.exp(scores - jnp.max(scores, axis=0, keepdims=True)).astype(BF))

    residual = x + jnp.dot(outw_ref[...], mixed[...], preferred_element_type=F32)
    normed_b = chan_norm(residual, gain_b_ref[...]).astype(BF)
    raised = jnp.dot(up_ref[...], normed_b, preferred_element_type=F32)
    hidden = (0.5 * raised * (1.0 + lax.erf(raised * 0.5**0.5))).astype(BF)
    return residual + jnp.dot(down_ref[...], hidden, preferred_element_type=F32)


def block_kernel(
    back, slot_ref, in_ref, qkv_ref, outw_ref, up_ref, down_ref, ga_ref, gb_ref, out_ref,
    source, rows, mixed,
):
    unpack_rows(in_ref, source)

    move_rows(2 * PACK, lambda i: source[pl.ds(i, 1), :], slot_ref, rows)

    def patch(p, _):
        at = pl.multiple_of(p * PATCH, PATCH)
        x = rows[pl.ds(at, PATCH), :].T[:C]
        y = patch_math(x, qkv_ref, outw_ref, up_ref, down_ref, ga_ref, gb_ref, mixed)
        if back:
            rows[pl.ds(at, PATCH), :] = jnp.concatenate([y, y], axis=0).T
        else:
            out_ref[:, pl.ds(at, PATCH)] = y.astype(BF)
        return 0

    lax.fori_loop(0, PTS // PATCH, patch, 0)
    if back:
        low_row = low_lanes(1)

        def fetch(g, _):
            at = g * UN
            taken = []
            for u in range(UN):
                low = rows[pl.ds(slot_ref[at + u], 1), :]
                high = rows[pl.ds(slot_ref[at + u + PACK], 1), :]
                taken.append(jnp.where(low_row, low, high))
            for u in range(UN):
                source[pl.ds(at + u, 1), :] = taken[u]
            return 0

        lax.fori_loop(0, PACK // UN, fetch, 0)
        out_ref[...] = source[0:PACK, :].astype(BF)


def block(back, slots, packed, qkv_w, out_w, up_w, down_w, gain_a, gain_b):
    out = (PACK, 128) if back else (C, PTS)
    return pl.pallas_call(
        functools.partial(block_kernel, back),
        in_specs=[pl.BlockSpec(memory_space=pltpu.SMEM)]
        + [pl.BlockSpec(memory_space=pltpu.VMEM)] * 7,
        out_specs=pl.BlockSpec(memory_space=pltpu.VMEM),
        out_shape=jax.ShapeDtypeStruct(out, BF),
        scratch_shapes=[
            pltpu.VMEM((2 * PACK, 128), F32),
            pltpu.VMEM((PTS + 8, 128), F32),
            pltpu.VMEM((C, PATCH), BF),
        ],
        compiler_params=pltpu.CompilerParams(vmem_limit_bytes=VMEM),
        cost_estimate=pl.CostEstimate(flops=4 * 10**10, bytes_accessed=10**6, transcendentals=0),
        name="block_back" if back else "block_last",
    )(slots, packed, qkv_w.T, out_w.T, up_w.T, down_w.T, gain_a[:, None], gain_b[:, None])


def beside(block_cols, sides, width):
    for axis, dim in sides:
        count = lax.axis_size(axis)
        forward = [(i, i + 1) for i in range(count - 1)]
        backward = [(target, source) for source, target in forward]
        low = lax.ppermute(block_cols[:, 1], axis, forward)
        high = lax.ppermute(block_cols[:, 0], axis, backward)
    return low, high


def places(dest):
    owners, slots = dest[0], dest[1]
    lanes = 128
    matches = (owners[None, :] == jnp.arange(DEV, dtype=jnp.int32)[:, None]).astype(BF)
    grouped = matches.reshape(DEV, PTS // lanes, lanes)
    index_row = jnp.arange(lanes, dtype=jnp.int32)
    strict = (index_row[:, None] < index_row[None, :]).astype(BF)
    within = jnp.einsum("dbi,ij->dbj", grouped, strict, preferred_element_type=F32)
    totals = jnp.sum(grouped.astype(F32), axis=2)
    before = jnp.cumsum(totals, axis=1) - totals
    ranking = jnp.sum(grouped.astype(F32) * (within + before[:, :, None]), axis=0)
    ranking = ranking.reshape(PTS).astype(jnp.int32)
    place = (ranking // HALF) * PACK + owners * HALF + ranking % HALF
    ranks = (ranking[:, None] == jnp.arange(CAP, dtype=jnp.int32)[None, :]).astype(BF)
    coded = slots + 1
    high = ranks * (coded // 64).astype(BF)[:, None]
    low = ranks * (coded % 64).astype(BF)[:, None]
    listed = jnp.dot(
        matches, jnp.concatenate([high, low], axis=1), preferred_element_type=F32
    ).astype(jnp.int32)
    listed = listed[:, :CAP] * 64 + listed[:, CAP:]
    return place, jnp.where(listed == 0, PTS, listed - 1)


def exchange(packed):
    shaped = packed.reshape(DEV, HALF, 128)
    moved = lax.all_to_all(shaped, ("gx", "gy"), split_axis=0, concat_axis=0, tiled=True)
    return moved.reshape(PACK, 128)


def local(
    feats,
    face_rows,
    neighbours,
    z_dest,
    h_dest,
    conv_weight,
    qkv_weight,
    out_weight,
    up_weight,
    down_weight,
    norm_gains,
):
    picked = jnp.take(feats, face_rows[0], axis=1)
    low_x, high_x = beside(picked[:, 0:2], (("gx", 1),), 1)
    low_y, high_y = beside(picked[:, 2:4], (("gy", 1),), 1)
    ext_rows = jnp.concatenate([feats, low_x, high_x, low_y, high_y], axis=1).T

    z_place, z_list = places(z_dest)
    h_place, h_list = places(h_dest)
    slots = lax.all_to_all(
        jnp.concatenate([z_list, h_list], axis=1), ("gx", "gy"),
        split_axis=0, concat_axis=0, tiled=True,
    )
    slots = slots.reshape(DEV, 4, HALF).transpose(1, 0, 2).reshape(2, 2 * PACK)

    others = jnp.concatenate([neighbours[:PAIRS], neighbours[PAIRS + 1 :]], axis=0)
    base = (jnp.arange(2 * PAIRS, dtype=jnp.int32) // 2 * TROWS)[:, None]
    idx = jnp.where(others < 0, EXT, others) + base
    idx = jnp.pad(idx, ((0, 1024 // GROUP - 2 * PAIRS), (0, 0)))
    idx = idx.reshape(1024, GROUPS).T.reshape(GROUPS, 8, 128)
    pair_w = jnp.concatenate([conv_weight[:PAIRS], conv_weight[PAIRS + 1 :]], axis=0)
    pair_w = jnp.concatenate([pair_w[0::2], pair_w[1::2]], axis=2)

    sent = conv_send(idx, z_place, ext_rows, pair_w, conv_weight[PAIRS], norm_gains[0:1])
    returned = block(
        True, slots[0], exchange(sent), qkv_weight[0], out_weight[0], up_weight[0],
        down_weight[0], norm_gains[1], norm_gains[2],
    )
    resent = relay(z_place, h_place, exchange(returned))
    return block(
        False, slots[1], exchange(resent), qkv_weight[1], out_weight[1], up_weight[1],
        down_weight[1], norm_gains[3], norm_gains[4],
    )


def solution(mesh):
    placed = (
        P(None, ("gx", "gy")),
        P(("gx", "gy"), None, None),
        P(None, ("gx", "gy")),
        P(None, ("gx", "gy")),
        P(None, ("gx", "gy")),
        P(),
        P(),
        P(),
        P(),
        P(),
        P(),
    )
    return jax.shard_map(
        local, mesh=mesh, in_specs=placed, out_specs=P(None, ("gx", "gy")), check_vma=False
    )
```

```python
import functools

import jax
import jax.numpy as jnp
from jax import lax
from jax.experimental import pallas as pl
from jax.experimental.pallas import tpu as pltpu
from jax.sharding import PartitionSpec as P

HEADS = 4
HEAD_DIM = 16
PATCH = 1024
C = 64
PTS = 4096
FACE = 128
EXT = PTS + 4 * FACE
TROWS = EXT + 8
DEV = 128
CAP = 48
HALF = CAP // 2
PACK = DEV * HALF
ON_CAP = 64
ON_HALF = ON_CAP // 2
EXTRA = 8
OUT_STRIDE = HALF + EXTRA
ON_STRIDE = ON_HALF + EXTRA
OUT_PACK = DEV * OUT_STRIDE
ON_PACK = DEV * ON_STRIDE
PAIRS = 13
BLK = 512
UN = 16
GROUP = 32
GROUPS = PTS // GROUP
LISTS = 4
LOG2_E = 1.4426950408889634
SAFE = 72.0
EPS = 1e-05
VMEM = 60 * 2**20
BF = jnp.bfloat16
F32 = jnp.float32


def lane_norm(values, gain):
    average = jnp.mean(values, axis=1, keepdims=True)
    centred = values - average
    spread = jnp.mean(centred * centred, axis=1, keepdims=True)
    return centred * lax.rsqrt(spread + EPS) * gain


def chan_norm(values, gain):
    average = jnp.mean(values, axis=0, keepdims=True)
    centred = values - average
    spread = jnp.mean(centred * centred, axis=0, keepdims=True)
    return centred * lax.rsqrt(spread + EPS) * gain


def low_lanes(rows):
    return lax.broadcasted_iota(jnp.int32, (rows, 128), 1) < C


def pack_rows(rows_ref, out_ref):
    count = out_ref.shape[0]

    def part(b, _):
        at = pl.multiple_of(b * 512, 512)
        low = rows_ref[pl.ds(at, 512), :]
        high = pltpu.roll(rows_ref[pl.ds(at + count, 512), :], C, 1)
        out_ref[pl.ds(at, 512), :] = jnp.where(low_lanes(512), low, high).astype(BF)
        return 0

    lax.fori_loop(0, count // 512, part, 0)


def unpack_rows(in_ref, rows_ref):
    count = in_ref.shape[0]

    def part(b, _):
        at = pl.multiple_of(b * 512, 512)
        both = in_ref[pl.ds(at, 512), :].astype(F32)
        rows_ref[pl.ds(at, 512), :] = both
        rows_ref[pl.ds(at + count, 512), :] = pltpu.roll(both, C, 1)
        return 0

    lax.fori_loop(0, count // 512, part, 0)


def move_rows(count, read, place_ref, rows_ref):
    def move(g, _):
        at = g * UN
        taken = [read(at + u) for u in range(UN)]
        for u in range(UN):
            rows_ref[pl.ds(place_ref[at + u], 1), :] = taken[u]
        return 0

    lax.fori_loop(0, count // UN, move, 0)


def put_codes(code_ref, rows_ref, half):
    def put(g, _):
        for u in range(8):
            d = g * 8 + u
            codes = code_ref[pl.ds(pl.multiple_of(d * EXTRA, EXTRA), EXTRA), :]
            at = pl.multiple_of(d * (half + EXTRA) + half, 8)
            rows_ref[pl.ds(at, EXTRA), :] = codes
        return 0

    lax.fori_loop(0, DEV // 8, put, 0)


def conv_kernel(
    near_ref, place_ref, code_ref, feats_ref, low_x, high_x, low_y, high_y, weight_ref, gain_ref,
    out_ref, *scratch,
):
    table, sums, rows, ext, orders = scratch[:5]
    lists, sems = scratch[5 : 5 + LISTS], scratch[5 + LISTS]

    def list_copy(g, b):
        return pltpu.make_async_copy(orders.at[g], lists[b], sems.at[b])

    offset = lax.broadcasted_iota(jnp.int32, (2 * PAIRS + 1, 128), 0)
    base = (offset - (offset > PAIRS).astype(jnp.int32)) // 2 * TROWS
    blank = jnp.zeros((32 - (2 * PAIRS + 1), 128), jnp.int32)
    for r in range(8):
        part = []
        for u in range(4 * r, 4 * r + 4):
            near = near_ref[:, u * 128 : (u + 1) * 128]
            part += [jnp.where(near < 0, EXT, near) + base, blank]
        orders[:, r, :] = jnp.concatenate(part, axis=0).T
    for b in range(LISTS):
        list_copy(b, b).start()

    def turn(b, _):
        at = pl.multiple_of(b * 512, 512)
        ext[pl.ds(at, 512), :] = feats_ref[:, pl.ds(at, 512)].astype(F32).T.astype(BF)
        return 0

    lax.fori_loop(0, PTS // 512, turn, 0)
    for i, face in enumerate((low_x, high_x, low_y, high_y)):
        ext[PTS + i * FACE : PTS + (i + 1) * FACE, :] = face[...].astype(F32).T.astype(BF)
    kept = [o for o in range(2 * PAIRS + 1) if o != PAIRS]
    pairs = [
        jnp.concatenate([weight_ref[kept[2 * j]], weight_ref[kept[2 * j + 1]]], axis=1)
        for j in range(PAIRS)
    ]

    def fill(b, _):
        at = pl.multiple_of(b * 512, 512)
        chunk = ext[pl.ds(at, 512), :]
        for j in range(PAIRS):
            table[pl.ds(pl.multiple_of(j * TROWS + at, 8), 512), :] = jnp.dot(
                chunk, pairs[j], preferred_element_type=F32
            )
        return 0

    lax.fori_loop(0, EXT // 512, fill, 0)
    for j in range(PAIRS):
        table[j * TROWS + EXT : (j + 1) * TROWS, :] = jnp.zeros((TROWS - EXT, 128), F32)

    low_row = low_lanes(1)

    def gather(step, _):
        for b in range(LISTS):
            g = step * LISTS + b
            list_copy(g, b).wait()
            for u in range(GROUP):
                even, odd = None, None
                for j in range(PAIRS):
                    at = u * 32 + kept[2 * j]
                    first = table[pl.ds(lists[b][at // 128, at % 128], 1), :]
                    at = u * 32 + kept[2 * j + 1]
                    second = table[pl.ds(lists[b][at // 128, at % 128], 1), :]
                    even = first if even is None else even + first
                    odd = second if odd is None else odd + second
                sums[pl.ds(u * GROUPS + g, 1), :] = jnp.where(low_row, even, odd)
            list_copy(jnp.minimum(g + LISTS, GROUPS - 1), b).start()
        return 0

    lax.fori_loop(0, GROUPS // LISTS, gather, 0)
    for b in range(LISTS):
        list_copy(GROUPS - 1, b).wait()

    def finish(b, _):
        at = pl.multiple_of(b * BLK, BLK)
        own = ext[pl.ds(at, BLK), :]
        both = sums[pl.ds(at, BLK), :]
        conv = both[:, :C] + both[:, C:] + jnp.dot(own, weight_ref[PAIRS], preferred_element_type=F32)
        sums[pl.ds(at, BLK), :C] = own.astype(F32) + lane_norm(conv, gain_ref[0:1, :])
        return 0

    lax.fori_loop(0, PTS // BLK, finish, 0)
    move_rows(PTS, lambda i: sums[pl.ds(i, 1), :], place_ref, rows)
    put_codes(code_ref, rows, HALF)
    pack_rows(rows, out_ref)


def conv_send(near, place, codes, feats, faces, weight, gains):
    return pl.pallas_call(
        conv_kernel,
        in_specs=[pl.BlockSpec(memory_space=pltpu.VMEM), pl.BlockSpec(memory_space=pltpu.SMEM)]
        + [pl.BlockSpec(memory_space=pltpu.VMEM)] * 8,
        out_specs=pl.BlockSpec(memory_space=pltpu.VMEM),
        out_shape=jax.ShapeDtypeStruct((OUT_PACK, 128), BF),
        scratch_shapes=[
            pltpu.VMEM((PAIRS * TROWS, 128), F32),
            pltpu.VMEM((PTS, 128), F32),
            pltpu.VMEM((2 * OUT_PACK, 128), F32),
            pltpu.VMEM((EXT, C), BF),
            pltpu.VMEM((GROUPS, 8, 128), jnp.int32),
        ]
        + [pltpu.SMEM((8, 128), jnp.int32)] * LISTS
        + [pltpu.SemaphoreType.DMA((LISTS,))],
        compiler_params=pltpu.CompilerParams(vmem_limit_bytes=VMEM),
        cost_estimate=pl.CostEstimate(flops=10**11, bytes_accessed=10**6, transcendentals=0),
        name="conv_send",
    )(near, place, codes, feats, *faces, weight, gains)


def relay_kernel(from_ref, to_ref, in_ref, out_ref, source, target):
    unpack_rows(in_ref, source)

    move_rows(PTS, lambda i: source[pl.ds(from_ref[i], 1), :], to_ref, target)
    pack_rows(target, out_ref)


def relay(place_from, place_to, packed):
    return pl.pallas_call(
        relay_kernel,
        in_specs=[
            pl.BlockSpec(memory_space=pltpu.SMEM),
            pl.BlockSpec(memory_space=pltpu.SMEM),
            pl.BlockSpec(memory_space=pltpu.VMEM),
        ],
        out_specs=pl.BlockSpec(memory_space=pltpu.VMEM),
        out_shape=jax.ShapeDtypeStruct((PACK, 128), BF),
        scratch_shapes=[
            pltpu.VMEM((2 * PACK, 128), F32),
            pltpu.VMEM((2 * PACK, 128), F32),
        ],
        compiler_params=pltpu.CompilerParams(vmem_limit_bytes=VMEM),
        cost_estimate=pl.CostEstimate(flops=10**9, bytes_accessed=10**6, transcendentals=0),
        name="relay",
    )(place_from, place_to, packed)


def turned_dot(weight, values):
    return lax.dot_general(
        weight, values, (((0,), (0,)), ((), ())), preferred_element_type=F32
    )


def patch_math(j, x, qkv_ref, outw_ref, up_ref, down_ref, gain_ref, mixed):
    normed = chan_norm(x, gain_ref[:, 2 * j + 1 : 2 * j + 2]).astype(BF)
    qkv = turned_dot(qkv_ref[j], normed).astype(BF)
    queries = qkv[:C].astype(F32)
    keys = qkv[C : 2 * C].astype(F32)
    keys_t = keys.T
    head_of = lax.broadcasted_iota(jnp.int32, (C, PATCH), 0) // HEAD_DIM
    ones = jnp.ones((HEAD_DIM, PATCH), BF)

    def of_head(h, values):
        return jnp.where(head_of == h, values, 0.0)

    def mix(h, weights):
        first = 2 * C + h * HEAD_DIM
        values = jnp.concatenate([qkv[first : first + HEAD_DIM], ones], axis=0)
        summed = jnp.dot(values, weights, preferred_element_type=F32)
        mixed[h * HEAD_DIM : (h + 1) * HEAD_DIM, :] = (
            summed[:HEAD_DIM] / summed[HEAD_DIM : HEAD_DIM + 1]
        ).astype(BF)

    def longest(values):
        squares = (values * values).reshape(HEADS, HEAD_DIM, PATCH)
        return jnp.max(jnp.sum(squares, axis=1), axis=1, keepdims=True)

    reach = jnp.max(longest(queries) * longest(keys))
    safe = reach <= (SAFE * HEAD_DIM**0.5) ** 2

    @pl.when(safe)
    def _():
        scaled = queries * (HEAD_DIM**-0.5 * LOG2_E)
        upper = scaled.astype(BF).astype(F32)
        lower = scaled - upper
        keys_2 = jnp.concatenate([keys_t, keys_t], axis=1).astype(BF)
        for h in range(HEADS):
            split = jnp.concatenate([of_head(h, upper), of_head(h, lower)], axis=0).astype(BF)
            scores = jnp.dot(keys_2, split, preferred_element_type=F32)
            mix(h, jnp.exp2(scores).astype(BF))

    @pl.when(jnp.logical_not(safe))
    def _():
        keys_1 = keys_t.astype(BF)
        for h in range(HEADS):
            one_head = of_head(h, queries * HEAD_DIM**-0.5).astype(BF)
            scores = jnp.dot(keys_1, one_head, preferred_element_type=F32)
            mix(h, jnp.exp(scores - jnp.max(scores, axis=0, keepdims=True)).astype(BF))

    residual = x + turned_dot(outw_ref[j], mixed[...])
    normed_b = chan_norm(residual, gain_ref[:, 2 * j + 2 : 2 * j + 3]).astype(BF)
    raised = turned_dot(up_ref[j], normed_b)
    hidden = (0.5 * raised * (1.0 + lax.erf(raised * 0.5**0.5))).astype(BF)
    return residual + turned_dot(down_ref[j], hidden)


def place_rows(half, slot_ref, in_ref, source, rows):
    unpack_rows(in_ref, source)
    count = in_ref.shape[0]
    stride = count // DEV

    def place(d, _):
        for side in range(2):
            at = side * count + d * stride
            taken = [source[pl.ds(at + k, 1), :] for k in range(half)]
            entry = d * 2 * half + side * half
            for k in range(half):
                rows[pl.ds(slot_ref[entry + k], 1), :] = taken[k]
        return 0

    lax.fori_loop(0, DEV, place, 0)


def first_kernel(
    slot_ref, onward_ref, in_ref, code_ref, qkv_ref, outw_ref, up_ref, down_ref, gain_ref,
    out_ref, done_ref, source, rows, mixed,
):
    place_rows(HALF, slot_ref, in_ref, source, rows)
    done_ref[PTS:, :] = jnp.zeros((8, 128), F32)

    def patch(p, _):
        at = pl.multiple_of(p * PATCH, PATCH)
        x = rows[pl.ds(at, PATCH), :].T[:C]
        y = patch_math(0, x, qkv_ref, outw_ref, up_ref, down_ref, gain_ref, mixed)
        y = y.astype(BF).astype(F32)
        done_ref[pl.ds(at, PATCH), :] = jnp.concatenate([y, y], axis=0).T
        return 0

    lax.fori_loop(0, PTS // PATCH, patch, 0)
    move_rows(DEV * CAP, lambda i: done_ref[pl.ds(slot_ref[i], 1), :], onward_ref, source)
    put_codes(code_ref, source, ON_HALF)
    pack_rows(source, out_ref)


def last_kernel(
    half, slot_ref, in_ref, qkv_ref, outw_ref, up_ref, down_ref, gain_ref,
    out_ref, source, rows, mixed,
):
    place_rows(half, slot_ref, in_ref, source, rows)

    def patch(p, _):
        at = pl.multiple_of(p * PATCH, PATCH)
        x = rows[pl.ds(at, PATCH), :].T[:C]
        y = patch_math(1, x, qkv_ref, outw_ref, up_ref, down_ref, gain_ref, mixed)
        out_ref[:, pl.ds(at, PATCH)] = y.astype(BF)
        return 0

    lax.fori_loop(0, PTS // PATCH, patch, 0)


def block_call(kernel, lists, operands, out_shape, buffer_rows, name):
    return pl.pallas_call(
        kernel,
        in_specs=[pl.BlockSpec(memory_space=pltpu.SMEM)] * len(lists)
        + [pl.BlockSpec(memory_space=pltpu.VMEM)] * len(operands),
        out_specs=jax.tree.map(lambda _: pl.BlockSpec(memory_space=pltpu.VMEM), out_shape),
        out_shape=out_shape,
        scratch_shapes=[
            pltpu.VMEM((buffer_rows, 128), F32),
            pltpu.VMEM((PTS + 8, 128), F32),
            pltpu.VMEM((C, PATCH), BF),
        ],
        compiler_params=pltpu.CompilerParams(vmem_limit_bytes=VMEM),
        cost_estimate=pl.CostEstimate(flops=4 * 10**10, bytes_accessed=10**6, transcendentals=0),
        name=name,
    )(*lists, *operands)


def first_block(slots, onward, packed, codes, weights):
    shapes = (
        jax.ShapeDtypeStruct((ON_PACK, 128), BF),
        jax.ShapeDtypeStruct((PTS + 8, 128), F32),
    )
    return block_call(
        first_kernel, (slots, onward), (packed, codes, *weights), shapes, 2 * ON_PACK + 8,
        "first_block",
    )


def last_block(half, slots, packed, weights):
    return block_call(
        functools.partial(last_kernel, half), (slots,), (packed, *weights),
        jax.ShapeDtypeStruct((C, PTS), BF), 2 * packed.shape[0], "last_block",
    )


def fetch_kernel(slot_ref, done_ref, out_ref, source):
    low_row = low_lanes(1)

    def fetch(g, _):
        at = g * UN
        taken = []
        for u in range(UN):
            low = done_ref[pl.ds(slot_ref[at + u], 1), :]
            high = done_ref[pl.ds(slot_ref[at + u + PACK], 1), :]
            taken.append(jnp.where(low_row, low, high))
        for u in range(UN):
            source[pl.ds(at + u, 1), :] = taken[u]
        return 0

    lax.fori_loop(0, PACK // UN, fetch, 0)
    out_ref[...] = source[...].astype(BF)


def fetch_back(slots, done):
    return pl.pallas_call(
        fetch_kernel,
        in_specs=[
            pl.BlockSpec(memory_space=pltpu.SMEM),
            pl.BlockSpec(memory_space=pltpu.VMEM),
        ],
        out_specs=pl.BlockSpec(memory_space=pltpu.VMEM),
        out_shape=jax.ShapeDtypeStruct((PACK, 128), BF),
        scratch_shapes=[pltpu.VMEM((PACK, 128), F32)],
        compiler_params=pltpu.CompilerParams(vmem_limit_bytes=VMEM),
        name="fetch_back",
    )(slots, done)


def beside(sides, axis):
    forward = [(i, i + 1) for i in range(lax.axis_size(axis) - 1)]
    backward = [(target, source) for source, target in forward]
    return [
        lax.ppermute(sides[:, 1], axis, forward),
        lax.ppermute(sides[:, 0], axis, backward),
    ]


def ranks_of(owners):
    lanes = 128
    count = owners.shape[0]
    matches = (owners[None, :] == jnp.arange(DEV, dtype=jnp.int32)[:, None]).astype(BF)
    grouped = matches.reshape(DEV, count // lanes, lanes)
    index_row = jnp.arange(lanes, dtype=jnp.int32)
    strict = (index_row[:, None] < index_row[None, :]).astype(BF)
    within = jnp.einsum("dbi,ij->dbj", grouped, strict, preferred_element_type=F32)
    totals = jnp.sum(grouped.astype(F32), axis=2)
    before = jnp.cumsum(totals, axis=1) - totals
    ranking = jnp.sum(grouped.astype(F32) * (within + before[:, :, None]), axis=0)
    return ranking.reshape(count).astype(jnp.int32), matches, jnp.max(jnp.sum(totals, axis=1))


def place_of(owners, ranking, half, stride):
    return (ranking // half) * (DEV * stride) + owners * stride + ranking % half


def listed(matches, ranking, capacity, pieces):
    ranks = (ranking[:, None] == jnp.arange(capacity, dtype=jnp.int32)[None, :]).astype(BF)
    columns = jnp.concatenate([ranks * piece.astype(BF)[:, None] for piece in pieces], axis=1)
    return jnp.dot(matches, columns, preferred_element_type=F32).reshape(DEV, -1, capacity)


def code_rows(lists):
    _, count, capacity = lists.shape
    padded = jnp.pad(lists, ((0, 0), (0, EXTRA - count), (0, 128 - capacity)))
    return padded.reshape(DEV * EXTRA, 128)


def read_codes(packed, half, capacity, count):
    rows = packed.reshape(DEV, half + EXTRA, 128)
    return rows[:, half : half + count, :capacity].astype(jnp.int32)


def slot_pieces(slots):
    return [(slots + 1) // 64, (slots + 1) % 64]


def as_slots(high, low):
    coded = high * 64 + low
    return jnp.where(coded == 0, PTS, coded - 1)


def swap(values):
    return lax.all_to_all(values, ("gx", "gy"), split_axis=0, concat_axis=0, tiled=True)


def exchange(packed):
    rows = packed.shape[0]
    return swap(packed.reshape(DEV, rows // DEV, 128)).reshape(rows, 128)


def through_home(z_slots, z_dest, z_ranking, h_dest, done, weights):
    ranking, matches, _ = ranks_of(h_dest[0])
    h_lists = listed(matches, ranking, CAP, slot_pieces(h_dest[1]))
    h_lists = swap(h_lists.astype(jnp.int32).reshape(DEV, 2 * CAP))
    h_slots = as_slots(h_lists[:, :CAP], h_lists[:, CAP:]).reshape(-1)
    back_slots = z_slots.reshape(DEV, 2, HALF).transpose(1, 0, 2).reshape(-1)
    returned = exchange(fetch_back(back_slots, done))
    z_place = place_of(z_dest[0], z_ranking, HALF, HALF)
    h_place = place_of(h_dest[0], ranking, HALF, HALF)
    resent = relay(z_place, h_place, returned)
    return last_block(HALF, h_slots, exchange(resent), weights)


def local(
    feats,
    face_rows,
    neighbours,
    z_dest,
    h_dest,
    conv_weight,
    qkv_weight,
    out_weight,
    up_weight,
    down_weight,
    norm_gains,
):
    picked = jnp.take(feats, face_rows[0], axis=1)
    faces = beside(picked[:, 0:2], "gx") + beside(picked[:, 2:4], "gy")

    z_ranking, matches, _ = ranks_of(z_dest[0])
    z_place = place_of(z_dest[0], z_ranking, HALF, OUT_STRIDE)
    pieces = slot_pieces(z_dest[1]) + [h_dest[0], h_dest[1] // 64, h_dest[1] % 64]
    codes = code_rows(listed(matches, z_ranking, CAP, pieces))
    received = exchange(
        conv_send(neighbours, z_place, codes, feats, faces, conv_weight, norm_gains)
    )

    codes = read_codes(received, HALF, CAP, 5)
    z_slots = as_slots(codes[:, 0], codes[:, 1]).reshape(-1)
    owners = jnp.where(z_slots == PTS, DEV, codes[:, 2].reshape(-1))
    ranking, matches, most = ranks_of(owners)
    kept = jnp.logical_and(owners < DEV, ranking < ON_CAP)
    onward = jnp.where(kept, place_of(owners, ranking, ON_HALF, ON_STRIDE), 2 * ON_PACK)
    next_slots = (codes[:, 3] * 64 + codes[:, 4]).reshape(-1)
    lists = listed(matches, ranking, ON_CAP, slot_pieces(next_slots))
    most = most.astype(jnp.int32)
    fullest = jnp.stack([most // 64, most % 64]).astype(F32)
    fullest = jnp.broadcast_to(fullest[None, :, None], (DEV, 2, ON_CAP))
    codes = code_rows(jnp.concatenate([lists, fullest], axis=1))

    weights = (qkv_weight, out_weight, up_weight, down_weight, norm_gains.T)
    direct, done = first_block(z_slots, onward, received, codes, weights)
    direct = exchange(direct)
    codes = read_codes(direct, ON_HALF, ON_CAP, 4)
    direct_slots = as_slots(codes[:, 0], codes[:, 1]).reshape(-1)
    fits = jnp.max(codes[:, 2, 0] * 64 + codes[:, 3, 0]) <= ON_CAP
    return lax.cond(
        fits,
        lambda: last_block(ON_HALF, direct_slots, direct, weights),
        lambda: through_home(z_slots, z_dest, z_ranking, h_dest, done, weights),
    )


def solution(mesh):
    placed = (
        P(None, ("gx", "gy")),
        P(("gx", "gy"), None, None),
        P(None, ("gx", "gy")),
        P(None, ("gx", "gy")),
        P(None, ("gx", "gy")),
        P(),
        P(),
        P(),
        P(),
        P(),
        P(),
    )
    return jax.shard_map(
        local, mesh=mesh, in_specs=placed, out_specs=P(None, ("gx", "gy")), check_vma=False
    )
```

```python
import functools

import jax
import jax.numpy as jnp
from jax import lax
from jax.experimental import pallas as pl
from jax.experimental.pallas import tpu as pltpu
from jax.sharding import PartitionSpec as P

HEADS = 4
HEAD_DIM = 16
PATCH = 1024
C = 64
PTS = 4096
FACE = 128
EXT = PTS + 4 * FACE
TROWS = EXT + 8
DEV = 128
CAP = 48
HALF = CAP // 2
PACK = DEV * HALF
ON_CAP = 64
ON_HALF = ON_CAP // 2
EXTRA = 8
OUT_STRIDE = HALF + EXTRA
ON_STRIDE = ON_HALF + EXTRA
OUT_PACK = DEV * OUT_STRIDE
ON_PACK = DEV * ON_STRIDE
PAIRS = 13
BLK = 512
UN = 16
GROUP = 32
GROUPS = PTS // GROUP
LISTS = 4
LOG2_E = 1.4426950408889634
SAFE = 72.0
EPS = 1e-05
VMEM = 60 * 2**20
BF = jnp.bfloat16
F32 = jnp.float32


def lane_norm(values, gain):
    average = jnp.mean(values, axis=1, keepdims=True)
    centred = values - average
    spread = jnp.mean(centred * centred, axis=1, keepdims=True)
    return centred * lax.rsqrt(spread + EPS) * gain


def chan_norm(values, gain):
    average = jnp.mean(values, axis=0, keepdims=True)
    centred = values - average
    spread = jnp.mean(centred * centred, axis=0, keepdims=True)
    return centred * lax.rsqrt(spread + EPS) * gain


def low_lanes(rows):
    return lax.broadcasted_iota(jnp.int32, (rows, 128), 1) < C


def pack_rows(rows_ref, out_ref):
    count = out_ref.shape[0]

    def part(b, _):
        at = pl.multiple_of(b * 512, 512)
        low = rows_ref[pl.ds(at, 512), :]
        high = pltpu.roll(rows_ref[pl.ds(at + count, 512), :], C, 1)
        out_ref[pl.ds(at, 512), :] = jnp.where(low_lanes(512), low, high).astype(BF)
        return 0

    lax.fori_loop(0, count // 512, part, 0)


def unpack_rows(in_ref, rows_ref):
    count = in_ref.shape[0]

    def part(b, _):
        at = pl.multiple_of(b * 512, 512)
        both = in_ref[pl.ds(at, 512), :].astype(F32)
        rows_ref[pl.ds(at, 512), :] = both
        rows_ref[pl.ds(at + count, 512), :] = pltpu.roll(both, C, 1)
        return 0

    lax.fori_loop(0, count // 512, part, 0)


def move_rows(count, read, place_ref, rows_ref):
    def move(g, _):
        at = g * UN
        taken = [read(at + u) for u in range(UN)]
        for u in range(UN):
            rows_ref[pl.ds(place_ref[at + u], 1), :] = taken[u]
        return 0

    lax.fori_loop(0, count // UN, move, 0)


def put_codes(code_ref, rows_ref, half):
    def put(g, _):
        for u in range(8):
            d = g * 8 + u
            codes = code_ref[pl.ds(pl.multiple_of(d * EXTRA, EXTRA), EXTRA), :]
            at = pl.multiple_of(d * (half + EXTRA) + half, 8)
            rows_ref[pl.ds(at, EXTRA), :] = codes
        return 0

    lax.fori_loop(0, DEV // 8, put, 0)


def conv_kernel(
    near_ref, place_ref, code_ref, feats_ref, low_x, high_x, low_y, high_y, weight_ref, gain_ref,
    out_ref, *scratch,
):
    table, sums, rows, ext, orders = scratch[:5]
    lists, sems = scratch[5 : 5 + LISTS], scratch[5 + LISTS]

    def list_copy(g, b):
        return pltpu.make_async_copy(orders.at[g], lists[b], sems.at[b])

    offset = lax.broadcasted_iota(jnp.int32, (2 * PAIRS + 1, 128), 0)
    base = (offset - (offset > PAIRS).astype(jnp.int32)) // 2 * TROWS
    blank = jnp.zeros((32 - (2 * PAIRS + 1), 128), jnp.int32)
    for r in range(8):
        part = []
        for u in range(4 * r, 4 * r + 4):
            near = near_ref[:, u * 128 : (u + 1) * 128]
            part += [jnp.where(near < 0, EXT, near) + base, blank]
        orders[:, r, :] = jnp.concatenate(part, axis=0).T
    for b in range(LISTS):
        list_copy(b, b).start()

    def turn(b, _):
        at = pl.multiple_of(b * 512, 512)
        ext[pl.ds(at, 512), :] = feats_ref[:, pl.ds(at, 512)].astype(F32).T.astype(BF)
        return 0

    lax.fori_loop(0, PTS // 512, turn, 0)
    for i, face in enumerate((low_x, high_x, low_y, high_y)):
        ext[PTS + i * FACE : PTS + (i + 1) * FACE, :] = face[...].astype(F32).T.astype(BF)
    kept = [o for o in range(2 * PAIRS + 1) if o != PAIRS]
    pairs = [
        jnp.concatenate([weight_ref[kept[2 * j]], weight_ref[kept[2 * j + 1]]], axis=1)
        for j in range(PAIRS)
    ]

    def fill(b, _):
        at = pl.multiple_of(b * 512, 512)
        chunk = ext[pl.ds(at, 512), :]
        for j in range(PAIRS):
            table[pl.ds(pl.multiple_of(j * TROWS + at, 8), 512), :] = jnp.dot(
                chunk, pairs[j], preferred_element_type=F32
            )
        return 0

    lax.fori_loop(0, EXT // 512, fill, 0)
    for j in range(PAIRS):
        table[j * TROWS + EXT : (j + 1) * TROWS, :] = jnp.zeros((TROWS - EXT, 128), F32)

    low_row = low_lanes(1)

    def gather(step, _):
        for b in range(LISTS):
            g = step * LISTS + b
            list_copy(g, b).wait()
            for u in range(GROUP):
                even, odd = None, None
                for j in range(PAIRS):
                    at = u * 32 + kept[2 * j]
                    first = table[pl.ds(lists[b][at // 128, at % 128], 1), :]
                    at = u * 32 + kept[2 * j + 1]
                    second = table[pl.ds(lists[b][at // 128, at % 128], 1), :]
                    even = first if even is None else even + first
                    odd = second if odd is None else odd + second
                sums[pl.ds(u * GROUPS + g, 1), :] = jnp.where(low_row, even, odd)
            list_copy(jnp.minimum(g + LISTS, GROUPS - 1), b).start()
        return 0

    lax.fori_loop(0, GROUPS // LISTS, gather, 0)
    for b in range(LISTS):
        list_copy(GROUPS - 1, b).wait()

    def finish(b, _):
        at = pl.multiple_of(b * BLK, BLK)
        own = ext[pl.ds(at, BLK), :]
        both = sums[pl.ds(at, BLK), :]
        conv = both[:, :C] + both[:, C:] + jnp.dot(own, weight_ref[PAIRS], preferred_element_type=F32)
        sums[pl.ds(at, BLK), :C] = own.astype(F32) + lane_norm(conv, gain_ref[0:1, :])
        return 0

    lax.fori_loop(0, PTS // BLK, finish, 0)
    move_rows(PTS, lambda i: sums[pl.ds(i, 1), :], place_ref, rows)
    put_codes(code_ref, rows, HALF)
    pack_rows(rows, out_ref)


def conv_send(near, place, codes, feats, faces, weight, gains):
    return pl.pallas_call(
        conv_kernel,
        in_specs=[pl.BlockSpec(memory_space=pltpu.VMEM), pl.BlockSpec(memory_space=pltpu.SMEM)]
        + [pl.BlockSpec(memory_space=pltpu.VMEM)] * 8,
        out_specs=pl.BlockSpec(memory_space=pltpu.VMEM),
        out_shape=jax.ShapeDtypeStruct((OUT_PACK, 128), BF),
        scratch_shapes=[
            pltpu.VMEM((PAIRS * TROWS, 128), F32),
            pltpu.VMEM((PTS, 128), F32),
            pltpu.VMEM((2 * OUT_PACK, 128), F32),
            pltpu.VMEM((EXT, C), BF),
            pltpu.VMEM((GROUPS, 8, 128), jnp.int32),
        ]
        + [pltpu.SMEM((8, 128), jnp.int32)] * LISTS
        + [pltpu.SemaphoreType.DMA((LISTS,))],
        compiler_params=pltpu.CompilerParams(vmem_limit_bytes=VMEM),
        cost_estimate=pl.CostEstimate(flops=10**11, bytes_accessed=10**6, transcendentals=0),
        name="conv_send",
    )(near, place, codes, feats, *faces, weight, gains)


def relay_kernel(from_ref, to_ref, in_ref, out_ref, source, target):
    unpack_rows(in_ref, source)

    move_rows(PTS, lambda i: source[pl.ds(from_ref[i], 1), :], to_ref, target)
    pack_rows(target, out_ref)


def relay(place_from, place_to, packed):
    return pl.pallas_call(
        relay_kernel,
        in_specs=[
            pl.BlockSpec(memory_space=pltpu.SMEM),
            pl.BlockSpec(memory_space=pltpu.SMEM),
            pl.BlockSpec(memory_space=pltpu.VMEM),
        ],
        out_specs=pl.BlockSpec(memory_space=pltpu.VMEM),
        out_shape=jax.ShapeDtypeStruct((PACK, 128), BF),
        scratch_shapes=[
            pltpu.VMEM((2 * PACK, 128), F32),
            pltpu.VMEM((2 * PACK, 128), F32),
        ],
        compiler_params=pltpu.CompilerParams(vmem_limit_bytes=VMEM),
        cost_estimate=pl.CostEstimate(flops=10**9, bytes_accessed=10**6, transcendentals=0),
        name="relay",
    )(place_from, place_to, packed)


def turned_dot(weight, values):
    return lax.dot_general(
        weight, values, (((0,), (0,)), ((), ())), preferred_element_type=F32
    )


def patch_math(j, x, qkv_ref, outw_ref, up_ref, down_ref, gain_ref, mixed, values_ref):
    normed = chan_norm(x, gain_ref[:, 2 * j + 1 : 2 * j + 2]).astype(BF)
    qkv = turned_dot(qkv_ref[j], normed).astype(BF)
    queries = qkv[:C].astype(F32)
    keys = qkv[C : 2 * C].astype(F32)
    keys_t = keys.T
    head_of = lax.broadcasted_iota(jnp.int32, (C, PATCH), 0) // HEAD_DIM
    ones = jnp.ones((HEAD_DIM, PATCH), BF)

    def of_head(h, values):
        return jnp.where(head_of == h, values, 0.0)

    def weighted(values, weights):
        summed = jnp.dot(
            jnp.concatenate([values, ones], axis=0), weights, preferred_element_type=F32
        )
        return (summed[:HEAD_DIM] / summed[HEAD_DIM : HEAD_DIM + 1]).astype(BF)

    def longest(values):
        squares = (values * values).reshape(HEADS, HEAD_DIM, PATCH)
        return jnp.max(jnp.sum(squares, axis=1), axis=1, keepdims=True)

    reach = jnp.max(longest(queries) * longest(keys))
    safe = reach <= (SAFE * HEAD_DIM**0.5) ** 2

    @pl.when(safe)
    def _():
        scaled = queries * (HEAD_DIM**-0.5 * LOG2_E)
        upper = scaled.astype(BF).astype(F32)
        lower = scaled - upper
        keys_2 = jnp.concatenate([keys_t, keys_t], axis=1).astype(BF)
        for h in range(HEADS):
            split = jnp.concatenate([of_head(h, upper), of_head(h, lower)], axis=0).astype(BF)
            scores = jnp.dot(keys_2, split, preferred_element_type=F32)
            first = h * HEAD_DIM
            values = qkv[2 * C + first : 2 * C + first + HEAD_DIM]
            mixed[first : first + HEAD_DIM, :] = weighted(values, jnp.exp2(scores).astype(BF))

    @pl.when(jnp.logical_not(safe))
    def _():
        keys_1 = keys_t.astype(BF)
        values_ref[...] = qkv[2 * C :]

        def head(h, _):
            one_head = of_head(h, queries * HEAD_DIM**-0.5).astype(BF)
            scores = jnp.dot(keys_1, one_head, preferred_element_type=F32)
            weights = jnp.exp(scores - jnp.max(scores, axis=0, keepdims=True)).astype(BF)
            at = pl.ds(pl.multiple_of(h * HEAD_DIM, HEAD_DIM), HEAD_DIM)
            mixed[at, :] = weighted(values_ref[at, :], weights)
            return 0

        lax.fori_loop(0, HEADS, head, 0)

    residual = x + turned_dot(outw_ref[j], mixed[...])
    normed_b = chan_norm(residual, gain_ref[:, 2 * j + 2 : 2 * j + 3]).astype(BF)
    raised = turned_dot(up_ref[j], normed_b)
    hidden = (0.5 * raised * (1.0 + lax.erf(raised * 0.5**0.5))).astype(BF)
    return residual + turned_dot(down_ref[j], hidden)


def place_rows(half, slot_ref, in_ref, source, rows):
    unpack_rows(in_ref, source)
    count = in_ref.shape[0]
    stride = count // DEV

    def place(d, _):
        for side in range(2):
            at = side * count + d * stride
            taken = [source[pl.ds(at + k, 1), :] for k in range(half)]
            entry = d * 2 * half + side * half
            for k in range(half):
                rows[pl.ds(slot_ref[entry + k], 1), :] = taken[k]
        return 0

    lax.fori_loop(0, DEV, place, 0)


def first_kernel(
    slot_ref, onward_ref, in_ref, code_ref, qkv_ref, outw_ref, up_ref, down_ref, gain_ref,
    out_ref, done_ref, source, rows, mixed, values_ref,
):
    place_rows(HALF, slot_ref, in_ref, source, rows)
    done_ref[PTS:, :] = jnp.zeros((8, 128), F32)

    def patch(p, _):
        at = pl.multiple_of(p * PATCH, PATCH)
        x = rows[pl.ds(at, PATCH), :].T[:C]
        y = patch_math(0, x, qkv_ref, outw_ref, up_ref, down_ref, gain_ref, mixed, values_ref)
        y = y.astype(BF).astype(F32)
        done_ref[pl.ds(at, PATCH), :] = jnp.concatenate([y, y], axis=0).T
        return 0

    lax.fori_loop(0, PTS // PATCH, patch, 0)
    move_rows(DEV * CAP, lambda i: done_ref[pl.ds(slot_ref[i], 1), :], onward_ref, source)
    put_codes(code_ref, source, ON_HALF)
    pack_rows(source, out_ref)


def last_kernel(
    half, slot_ref, in_ref, qkv_ref, outw_ref, up_ref, down_ref, gain_ref,
    out_ref, source, rows, mixed, values_ref,
):
    place_rows(half, slot_ref, in_ref, source, rows)

    def patch(p, _):
        at = pl.multiple_of(p * PATCH, PATCH)
        x = rows[pl.ds(at, PATCH), :].T[:C]
        y = patch_math(1, x, qkv_ref, outw_ref, up_ref, down_ref, gain_ref, mixed, values_ref)
        out_ref[:, pl.ds(at, PATCH)] = y.astype(BF)
        return 0

    lax.fori_loop(0, PTS // PATCH, patch, 0)


def block_call(kernel, lists, operands, out_shape, buffer_rows, name):
    return pl.pallas_call(
        kernel,
        in_specs=[pl.BlockSpec(memory_space=pltpu.SMEM)] * len(lists)
        + [pl.BlockSpec(memory_space=pltpu.VMEM)] * len(operands),
        out_specs=jax.tree.map(lambda _: pl.BlockSpec(memory_space=pltpu.VMEM), out_shape),
        out_shape=out_shape,
        scratch_shapes=[
            pltpu.VMEM((buffer_rows, 128), F32),
            pltpu.VMEM((PTS + 8, 128), F32),
            pltpu.VMEM((C, PATCH), BF),
            pltpu.VMEM((C, PATCH), BF),
        ],
        compiler_params=pltpu.CompilerParams(vmem_limit_bytes=VMEM),
        cost_estimate=pl.CostEstimate(flops=4 * 10**10, bytes_accessed=10**6, transcendentals=0),
        name=name,
    )(*lists, *operands)


def first_block(slots, onward, packed, codes, weights):
    shapes = (
        jax.ShapeDtypeStruct((ON_PACK, 128), BF),
        jax.ShapeDtypeStruct((PTS + 8, 128), F32),
    )
    return block_call(
        first_kernel, (slots, onward), (packed, codes, *weights), shapes, 2 * ON_PACK + 8,
        "first_block",
    )


def last_block(half, slots, packed, weights):
    return block_call(
        functools.partial(last_kernel, half), (slots,), (packed, *weights),
        jax.ShapeDtypeStruct((C, PTS), BF), 2 * packed.shape[0], "last_block",
    )


def fetch_kernel(slot_ref, done_ref, out_ref, source):
    low_row = low_lanes(1)

    def fetch(g, _):
        at = g * UN
        taken = []
        for u in range(UN):
            low = done_ref[pl.ds(slot_ref[at + u], 1), :]
            high = done_ref[pl.ds(slot_ref[at + u + PACK], 1), :]
            taken.append(jnp.where(low_row, low, high))
        for u in range(UN):
            source[pl.ds(at + u, 1), :] = taken[u]
        return 0

    lax.fori_loop(0, PACK // UN, fetch, 0)
    out_ref[...] = source[...].astype(BF)


def fetch_back(slots, done):
    return pl.pallas_call(
        fetch_kernel,
        in_specs=[
            pl.BlockSpec(memory_space=pltpu.SMEM),
            pl.BlockSpec(memory_space=pltpu.VMEM),
        ],
        out_specs=pl.BlockSpec(memory_space=pltpu.VMEM),
        out_shape=jax.ShapeDtypeStruct((PACK, 128), BF),
        scratch_shapes=[pltpu.VMEM((PACK, 128), F32)],
        compiler_params=pltpu.CompilerParams(vmem_limit_bytes=VMEM),
        name="fetch_back",
    )(slots, done)


def beside(sides, axis):
    forward = [(i, i + 1) for i in range(lax.axis_size(axis) - 1)]
    backward = [(target, source) for source, target in forward]
    return [
        lax.ppermute(sides[:, 1], axis, forward),
        lax.ppermute(sides[:, 0], axis, backward),
    ]


def ranks_of(owners):
    lanes = 128
    count = owners.shape[0]
    matches = (owners[None, :] == jnp.arange(DEV, dtype=jnp.int32)[:, None]).astype(BF)
    grouped = matches.reshape(DEV, count // lanes, lanes)
    index_row = jnp.arange(lanes, dtype=jnp.int32)
    strict = (index_row[:, None] < index_row[None, :]).astype(BF)
    within = jnp.einsum("dbi,ij->dbj", grouped, strict, preferred_element_type=F32)
    totals = jnp.sum(grouped.astype(F32), axis=2)
    before = jnp.cumsum(totals, axis=1) - totals
    ranking = jnp.sum(grouped.astype(F32) * (within + before[:, :, None]), axis=0)
    return ranking.reshape(count).astype(jnp.int32), matches, jnp.max(jnp.sum(totals, axis=1))


def place_of(owners, ranking, half, stride):
    return (ranking // half) * (DEV * stride) + owners * stride + ranking % half


def listed(matches, ranking, capacity, pieces):
    ranks = (ranking[:, None] == jnp.arange(capacity, dtype=jnp.int32)[None, :]).astype(BF)
    columns = jnp.concatenate([ranks * piece.astype(BF)[:, None] for piece in pieces], axis=1)
    return jnp.dot(matches, columns, preferred_element_type=F32).reshape(DEV, -1, capacity)


def code_rows(lists):
    _, count, capacity = lists.shape
    padded = jnp.pad(lists, ((0, 0), (0, EXTRA - count), (0, 128 - capacity)))
    return padded.reshape(DEV * EXTRA, 128)


def read_codes(packed, half, capacity, count):
    rows = packed.reshape(DEV, half + EXTRA, 128)
    return rows[:, half : half + count, :capacity].astype(jnp.int32)


def slot_pieces(slots):
    return [(slots + 1) // 64, (slots + 1) % 64]


def as_slots(high, low):
    coded = high * 64 + low
    return jnp.where(coded == 0, PTS, coded - 1)


def swap(values):
    return lax.all_to_all(values, ("gx", "gy"), split_axis=0, concat_axis=0, tiled=True)


def exchange(packed):
    rows = packed.shape[0]
    return swap(packed.reshape(DEV, rows // DEV, 128)).reshape(rows, 128)


def through_home(z_slots, z_dest, z_ranking, h_dest, done, weights):
    ranking, matches, _ = ranks_of(h_dest[0])
    h_lists = listed(matches, ranking, CAP, slot_pieces(h_dest[1]))
    h_lists = swap(h_lists.astype(jnp.int32).reshape(DEV, 2 * CAP))
    h_slots = as_slots(h_lists[:, :CAP], h_lists[:, CAP:]).reshape(-1)
    back_slots = z_slots.reshape(DEV, 2, HALF).transpose(1, 0, 2).reshape(-1)
    returned = exchange(fetch_back(back_slots, done))
    z_place = place_of(z_dest[0], z_ranking, HALF, HALF)
    h_place = place_of(h_dest[0], ranking, HALF, HALF)
    resent = relay(z_place, h_place, returned)
    return last_block(HALF, h_slots, exchange(resent), weights)


def local(
    feats,
    face_rows,
    neighbours,
    z_dest,
    h_dest,
    conv_weight,
    qkv_weight,
    out_weight,
    up_weight,
    down_weight,
    norm_gains,
):
    picked = jnp.take(feats, face_rows[0], axis=1)
    faces = beside(picked[:, 0:2], "gx") + beside(picked[:, 2:4], "gy")

    z_ranking, matches, _ = ranks_of(z_dest[0])
    z_place = place_of(z_dest[0], z_ranking, HALF, OUT_STRIDE)
    pieces = slot_pieces(z_dest[1]) + [h_dest[0], h_dest[1] // 64, h_dest[1] % 64]
    codes = code_rows(listed(matches, z_ranking, CAP, pieces))
    received = exchange(
        conv_send(neighbours, z_place, codes, feats, faces, conv_weight, norm_gains)
    )

    codes = read_codes(received, HALF, CAP, 5)
    z_slots = as_slots(codes[:, 0], codes[:, 1]).reshape(-1)
    owners = jnp.where(z_slots == PTS, DEV, codes[:, 2].reshape(-1))
    ranking, matches, most = ranks_of(owners)
    kept = jnp.logical_and(owners < DEV, ranking < ON_CAP)
    onward = jnp.where(kept, place_of(owners, ranking, ON_HALF, ON_STRIDE), 2 * ON_PACK)
    next_slots = (codes[:, 3] * 64 + codes[:, 4]).reshape(-1)
    lists = listed(matches, ranking, ON_CAP, slot_pieces(next_slots))
    most = most.astype(jnp.int32)
    fullest = jnp.stack([most // 64, most % 64]).astype(F32)
    fullest = jnp.broadcast_to(fullest[None, :, None], (DEV, 2, ON_CAP))
    codes = code_rows(jnp.concatenate([lists, fullest], axis=1))

    weights = (qkv_weight, out_weight, up_weight, down_weight, norm_gains.T)
    direct, done = first_block(z_slots, onward, received, codes, weights)
    direct = exchange(direct)
    codes = read_codes(direct, ON_HALF, ON_CAP, 4)
    direct_slots = as_slots(codes[:, 0], codes[:, 1]).reshape(-1)
    fits = jnp.max(codes[:, 2, 0] * 64 + codes[:, 3, 0]) <= ON_CAP
    return lax.cond(
        fits,
        lambda: last_block(ON_HALF, direct_slots, direct, weights),
        lambda: through_home(z_slots, z_dest, z_ranking, h_dest, done, weights),
    )


def solution(mesh):
    placed = (
        P(None, ("gx", "gy")),
        P(("gx", "gy"), None, None),
        P(None, ("gx", "gy")),
        P(None, ("gx", "gy")),
        P(None, ("gx", "gy")),
        P(),
        P(),
        P(),
        P(),
        P(),
        P(),
    )
    return jax.shard_map(
        local, mesh=mesh, in_specs=placed, out_specs=P(None, ("gx", "gy")), check_vma=False
    )
```

```python
import functools

import jax
import jax.numpy as jnp
from jax import lax
from jax.experimental import pallas as pl
from jax.experimental.pallas import tpu as pltpu
from jax.sharding import PartitionSpec as P

HEADS = 4
HEAD_DIM = 16
PATCH = 1024
C = 64
PTS = 4096
FACE = 128
EXT = PTS + 4 * FACE
TROWS = EXT + 8
DEV = 128
CAP = 48
HALF = CAP // 2
PACK = DEV * HALF
ON_CAP = 64
ON_HALF = ON_CAP // 2
EXTRA = 8
OUT_STRIDE = HALF + EXTRA
ON_STRIDE = ON_HALF + EXTRA
OUT_PACK = DEV * OUT_STRIDE
ON_PACK = DEV * ON_STRIDE
PAIRS = 13
BLK = 512
UN = 64
GROUP = 32
GROUPS = PTS // GROUP
LISTS = 4
LOG2_E = 1.4426950408889634
SAFE = 72.0
EPS = 1e-05
VMEM = 60 * 2**20
BF = jnp.bfloat16
F32 = jnp.float32


def lane_norm(values, gain):
    average = jnp.mean(values, axis=1, keepdims=True)
    centred = values - average
    spread = jnp.mean(centred * centred, axis=1, keepdims=True)
    return centred * lax.rsqrt(spread + EPS) * gain


def chan_norm(values, gain):
    average = jnp.mean(values, axis=0, keepdims=True)
    centred = values - average
    spread = jnp.mean(centred * centred, axis=0, keepdims=True)
    return centred * lax.rsqrt(spread + EPS) * gain


def low_lanes(rows):
    return lax.broadcasted_iota(jnp.int32, (rows, 128), 1) < C


def pack_rows(rows_ref, out_ref):
    count = out_ref.shape[0]

    def part(b, _):
        at = pl.multiple_of(b * 512, 512)
        low = rows_ref[pl.ds(at, 512), :]
        high = pltpu.roll(rows_ref[pl.ds(at + count, 512), :], C, 1)
        out_ref[pl.ds(at, 512), :] = jnp.where(low_lanes(512), low, high).astype(BF)
        return 0

    lax.fori_loop(0, count // 512, part, 0)


def unpack_rows(in_ref, rows_ref):
    count = in_ref.shape[0]

    def part(b, _):
        at = pl.multiple_of(b * 512, 512)
        both = in_ref[pl.ds(at, 512), :].astype(F32)
        rows_ref[pl.ds(at, 512), :] = both
        rows_ref[pl.ds(at + count, 512), :] = pltpu.roll(both, C, 1)
        return 0

    lax.fori_loop(0, count // 512, part, 0)


def move_rows(count, read, place_ref, rows_ref):
    def move(g, _):
        at = g * UN
        taken = [read(at + u) for u in range(UN)]
        for u in range(UN):
            rows_ref[pl.ds(place_ref[at + u], 1), :] = taken[u]
        return 0

    lax.fori_loop(0, count // UN, move, 0)


def put_codes(code_ref, rows_ref, half):
    def put(g, _):
        for u in range(8):
            d = g * 8 + u
            codes = code_ref[pl.ds(pl.multiple_of(d * EXTRA, EXTRA), EXTRA), :]
            at = pl.multiple_of(d * (half + EXTRA) + half, 8)
            rows_ref[pl.ds(at, EXTRA), :] = codes
        return 0

    lax.fori_loop(0, DEV // 8, put, 0)


def conv_kernel(
    near_ref, place_ref, code_ref, feats_ref, low_x, high_x, low_y, high_y, weight_ref, gain_ref,
    out_ref, *scratch,
):
    table, sums, rows, ext, orders = scratch[:5]
    lists, sems = scratch[5 : 5 + LISTS], scratch[5 + LISTS]

    def list_copy(g, b):
        return pltpu.make_async_copy(orders.at[g], lists[b], sems.at[b])

    offset = lax.broadcasted_iota(jnp.int32, (2 * PAIRS + 1, 128), 0)
    base = (offset - (offset > PAIRS).astype(jnp.int32)) // 2 * TROWS
    blank = jnp.zeros((32 - (2 * PAIRS + 1), 128), jnp.int32)
    for r in range(8):
        part = []
        for u in range(4 * r, 4 * r + 4):
            near = near_ref[:, u * 128 : (u + 1) * 128]
            part += [jnp.where(near < 0, EXT, near) + base, blank]
        orders[:, r, :] = jnp.concatenate(part, axis=0).T
    for b in range(LISTS):
        list_copy(b, b).start()

    def turn(b, _):
        at = pl.multiple_of(b * 512, 512)
        ext[pl.ds(at, 512), :] = feats_ref[:, pl.ds(at, 512)].astype(F32).T.astype(BF)
        return 0

    lax.fori_loop(0, PTS // 512, turn, 0)
    for i, face in enumerate((low_x, high_x, low_y, high_y)):
        ext[PTS + i * FACE : PTS + (i + 1) * FACE, :] = face[...].astype(F32).T.astype(BF)
    kept = [o for o in range(2 * PAIRS + 1) if o != PAIRS]
    pairs = [
        jnp.concatenate([weight_ref[kept[2 * j]], weight_ref[kept[2 * j + 1]]], axis=1)
        for j in range(PAIRS)
    ]

    def fill(b, _):
        at = pl.multiple_of(b * 512, 512)
        chunk = ext[pl.ds(at, 512), :]
        for j in range(PAIRS):
            table[pl.ds(pl.multiple_of(j * TROWS + at, 8), 512), :] = jnp.dot(
                chunk, pairs[j], preferred_element_type=F32
            )
        return 0

    lax.fori_loop(0, EXT // 512, fill, 0)
    for j in range(PAIRS):
        table[j * TROWS + EXT : (j + 1) * TROWS, :] = jnp.zeros((TROWS - EXT, 128), F32)

    low_row = low_lanes(1)

    def gather(step, _):
        for b in range(LISTS):
            g = step * LISTS + b
            list_copy(g, b).wait()
            for u in range(GROUP):
                even, odd = None, None
                for j in range(PAIRS):
                    at = u * 32 + kept[2 * j]
                    first = table[pl.ds(lists[b][at // 128, at % 128], 1), :]
                    at = u * 32 + kept[2 * j + 1]
                    second = table[pl.ds(lists[b][at // 128, at % 128], 1), :]
                    even = first if even is None else even + first
                    odd = second if odd is None else odd + second
                sums[pl.ds(u * GROUPS + g, 1), :] = jnp.where(low_row, even, odd)
            list_copy(jnp.minimum(g + LISTS, GROUPS - 1), b).start()
        return 0

    lax.fori_loop(0, GROUPS // LISTS, gather, 0)
    for b in range(LISTS):
        list_copy(GROUPS - 1, b).wait()

    def finish(b, _):
        at = pl.multiple_of(b * BLK, BLK)
        own = ext[pl.ds(at, BLK), :]
        both = sums[pl.ds(at, BLK), :]
        conv = both[:, :C] + both[:, C:] + jnp.dot(own, weight_ref[PAIRS], preferred_element_type=F32)
        sums[pl.ds(at, BLK), :C] = own.astype(F32) + lane_norm(conv, gain_ref[0:1, :])
        return 0

    lax.fori_loop(0, PTS // BLK, finish, 0)
    move_rows(PTS, lambda i: sums[pl.ds(i, 1), :], place_ref, rows)
    put_codes(code_ref, rows, HALF)
    pack_rows(rows, out_ref)


def conv_send(near, place, codes, feats, faces, weight, gains):
    return pl.pallas_call(
        conv_kernel,
        in_specs=[pl.BlockSpec(memory_space=pltpu.VMEM), pl.BlockSpec(memory_space=pltpu.SMEM)]
        + [pl.BlockSpec(memory_space=pltpu.VMEM)] * 8,
        out_specs=pl.BlockSpec(memory_space=pltpu.VMEM),
        out_shape=jax.ShapeDtypeStruct((OUT_PACK, 128), BF),
        scratch_shapes=[
            pltpu.VMEM((PAIRS * TROWS, 128), F32),
            pltpu.VMEM((PTS, 128), F32),
            pltpu.VMEM((2 * OUT_PACK, 128), F32),
            pltpu.VMEM((EXT, C), BF),
            pltpu.VMEM((GROUPS, 8, 128), jnp.int32),
        ]
        + [pltpu.SMEM((8, 128), jnp.int32)] * LISTS
        + [pltpu.SemaphoreType.DMA((LISTS,))],
        compiler_params=pltpu.CompilerParams(vmem_limit_bytes=VMEM),
        cost_estimate=pl.CostEstimate(flops=10**11, bytes_accessed=10**6, transcendentals=0),
        name="conv_send",
    )(near, place, codes, feats, *faces, weight, gains)


def relay_kernel(from_ref, to_ref, in_ref, out_ref, source, target):
    unpack_rows(in_ref, source)

    move_rows(PTS, lambda i: source[pl.ds(from_ref[i], 1), :], to_ref, target)
    pack_rows(target, out_ref)


def relay(place_from, place_to, packed):
    return pl.pallas_call(
        relay_kernel,
        in_specs=[
            pl.BlockSpec(memory_space=pltpu.SMEM),
            pl.BlockSpec(memory_space=pltpu.SMEM),
            pl.BlockSpec(memory_space=pltpu.VMEM),
        ],
        out_specs=pl.BlockSpec(memory_space=pltpu.VMEM),
        out_shape=jax.ShapeDtypeStruct((PACK, 128), BF),
        scratch_shapes=[
            pltpu.VMEM((2 * PACK, 128), F32),
            pltpu.VMEM((2 * PACK, 128), F32),
        ],
        compiler_params=pltpu.CompilerParams(vmem_limit_bytes=VMEM),
        cost_estimate=pl.CostEstimate(flops=10**9, bytes_accessed=10**6, transcendentals=0),
        name="relay",
    )(place_from, place_to, packed)


def turned_dot(weight, values):
    return lax.dot_general(
        weight, values, (((0,), (0,)), ((), ())), preferred_element_type=F32
    )


def patch_math(j, x, qkv_ref, outw_ref, up_ref, down_ref, gain_ref, mixed, values_ref):
    normed = chan_norm(x, gain_ref[:, 2 * j + 1 : 2 * j + 2]).astype(BF)
    qkv = turned_dot(qkv_ref[j], normed).astype(BF)
    queries = qkv[:C].astype(F32)
    keys = qkv[C : 2 * C].astype(F32)
    keys_t = keys.T
    head_of = lax.broadcasted_iota(jnp.int32, (C, PATCH), 0) // HEAD_DIM
    ones = jnp.ones((HEAD_DIM, PATCH), BF)

    def of_head(h, values):
        return jnp.where(head_of == h, values, 0.0)

    def weighted(values, weights):
        summed = jnp.dot(
            jnp.concatenate([values, ones], axis=0), weights, preferred_element_type=F32
        )
        return (summed[:HEAD_DIM] / summed[HEAD_DIM : HEAD_DIM + 1]).astype(BF)

    def longest(values):
        squares = (values * values).reshape(HEADS, HEAD_DIM, PATCH)
        return jnp.max(jnp.sum(squares, axis=1), axis=1, keepdims=True)

    reach = jnp.max(longest(queries) * longest(keys))
    safe = reach <= (SAFE * HEAD_DIM**0.5) ** 2

    @pl.when(safe)
    def _():
        scaled = queries * (HEAD_DIM**-0.5 * LOG2_E)
        upper = scaled.astype(BF).astype(F32)
        lower = scaled - upper
        keys_2 = jnp.concatenate([keys_t, keys_t], axis=1).astype(BF)
        for h in range(HEADS):
            split = jnp.concatenate([of_head(h, upper), of_head(h, lower)], axis=0).astype(BF)
            scores = jnp.dot(keys_2, split, preferred_element_type=F32)
            first = h * HEAD_DIM
            values = qkv[2 * C + first : 2 * C + first + HEAD_DIM]
            mixed[first : first + HEAD_DIM, :] = weighted(values, jnp.exp2(scores).astype(BF))

    @pl.when(jnp.logical_not(safe))
    def _():
        keys_1 = keys_t.astype(BF)
        values_ref[...] = qkv[2 * C :]

        def head(h, _):
            one_head = of_head(h, queries * HEAD_DIM**-0.5).astype(BF)
            scores = jnp.dot(keys_1, one_head, preferred_element_type=F32)
            weights = jnp.exp(scores - jnp.max(scores, axis=0, keepdims=True)).astype(BF)
            at = pl.ds(pl.multiple_of(h * HEAD_DIM, HEAD_DIM), HEAD_DIM)
            mixed[at, :] = weighted(values_ref[at, :], weights)
            return 0

        lax.fori_loop(0, HEADS, head, 0)

    residual = x + turned_dot(outw_ref[j], mixed[...])
    normed_b = chan_norm(residual, gain_ref[:, 2 * j + 2 : 2 * j + 3]).astype(BF)
    raised = turned_dot(up_ref[j], normed_b)
    hidden = (0.5 * raised * (1.0 + lax.erf(raised * 0.5**0.5))).astype(BF)
    return residual + turned_dot(down_ref[j], hidden)


def place_rows(half, span, slot_ref, in_ref, source, rows):
    unpack_rows(in_ref, source)
    count = in_ref.shape[0]
    stride = count // DEV

    def place(d, _):
        for side in range(2):
            at = side * count + d * stride
            taken = [source[pl.ds(at + k, 1), :] for k in range(half)]
            entry = d * span + side * half
            for k in range(half):
                rows[pl.ds(slot_ref[entry + k], 1), :] = taken[k]
        return 0

    lax.fori_loop(0, DEV, place, 0)


def first_kernel(
    slot_ref, onward_ref, in_ref, code_ref, qkv_ref, outw_ref, up_ref, down_ref, gain_ref,
    out_ref, done_ref, source, rows, mixed, values_ref,
):
    place_rows(HALF, 128, slot_ref, in_ref, source, rows)
    done_ref[PTS:, :] = jnp.zeros((8, 128), F32)

    def patch(p, _):
        at = pl.multiple_of(p * PATCH, PATCH)
        x = rows[pl.ds(at, PATCH), :].T[:C]
        y = patch_math(0, x, qkv_ref, outw_ref, up_ref, down_ref, gain_ref, mixed, values_ref)
        y = y.astype(BF).astype(F32)
        done_ref[pl.ds(at, PATCH), :] = jnp.concatenate([y, y], axis=0).T
        return 0

    lax.fori_loop(0, PTS // PATCH, patch, 0)

    def send(d, _):
        for side in range(2):
            entry = d * 128 + side * HALF
            taken = [done_ref[pl.ds(slot_ref[entry + k], 1), :] for k in range(HALF)]
            for k in range(HALF):
                source[pl.ds(onward_ref[entry + k], 1), :] = taken[k]
        return 0

    lax.fori_loop(0, DEV, send, 0)
    put_codes(code_ref, source, ON_HALF)
    pack_rows(source, out_ref)


def last_kernel(
    half, slot_ref, in_ref, qkv_ref, outw_ref, up_ref, down_ref, gain_ref,
    out_ref, source, rows, mixed, values_ref,
):
    place_rows(half, 2 * half, slot_ref, in_ref, source, rows)

    def patch(p, _):
        at = pl.multiple_of(p * PATCH, PATCH)
        x = rows[pl.ds(at, PATCH), :].T[:C]
        y = patch_math(1, x, qkv_ref, outw_ref, up_ref, down_ref, gain_ref, mixed, values_ref)
        out_ref[:, pl.ds(at, PATCH)] = y.astype(BF)
        return 0

    lax.fori_loop(0, PTS // PATCH, patch, 0)


def block_call(kernel, lists, operands, out_shape, buffer_rows, name):
    return pl.pallas_call(
        kernel,
        in_specs=[pl.BlockSpec(memory_space=pltpu.SMEM)] * len(lists)
        + [pl.BlockSpec(memory_space=pltpu.VMEM)] * len(operands),
        out_specs=jax.tree.map(lambda _: pl.BlockSpec(memory_space=pltpu.VMEM), out_shape),
        out_shape=out_shape,
        scratch_shapes=[
            pltpu.VMEM((buffer_rows, 128), F32),
            pltpu.VMEM((PTS + 8, 128), F32),
            pltpu.VMEM((C, PATCH), BF),
            pltpu.VMEM((C, PATCH), BF),
        ],
        compiler_params=pltpu.CompilerParams(vmem_limit_bytes=VMEM),
        cost_estimate=pl.CostEstimate(flops=4 * 10**10, bytes_accessed=10**6, transcendentals=0),
        name=name,
    )(*lists, *operands)


def first_block(slots, onward, packed, codes, weights):
    shapes = (
        jax.ShapeDtypeStruct((ON_PACK, 128), BF),
        jax.ShapeDtypeStruct((PTS + 8, 128), F32),
    )
    return block_call(
        first_kernel, (slots, onward), (packed, codes, *weights), shapes, 2 * ON_PACK + 8,
        "first_block",
    )


def last_block(half, slots, packed, weights):
    return block_call(
        functools.partial(last_kernel, half), (slots,), (packed, *weights),
        jax.ShapeDtypeStruct((C, PTS), BF), 2 * packed.shape[0], "last_block",
    )


def plan_kernel(in_ref, slot_ref, onward_ref, code_ref, mine, turned, marks, picks):
    def take(d, _):
        tile = in_ref[pl.ds(pl.multiple_of(d * OUT_STRIDE + HALF - EXTRA, 16), 16), :]
        mine[pl.ds(pl.multiple_of(d * EXTRA, EXTRA), EXTRA), :] = tile.astype(F32)[EXTRA:]
        return 0

    lax.fori_loop(0, DEV, take, 0, unroll=8)
    high, low, owner, next_high, next_low = (
        mine[pl.ds(p, DEV, stride=EXTRA), :] for p in range(5)
    )
    coded = (high * 64.0 + low).astype(jnp.int32)
    slot_ref[...] = jnp.where(coded == 0, PTS, coded - 1)
    owners = jnp.where(coded == 0, float(DEV), owner)
    following = (next_high * 64.0 + next_low).astype(jnp.int32) + 1
    turned[0] = owners.T
    turned[1] = jnp.zeros((DEV, 128), F32)
    turned[2] = (following >> 6).astype(F32).T
    turned[3] = (following & 63).astype(F32).T
    row = lax.broadcasted_iota(jnp.int32, (DEV, 128), 0)
    row_f = row.astype(F32)
    ahead = (row < lax.broadcasted_iota(jnp.int32, (DEV, 128), 1)).astype(F32).astype(BF)

    def matches(r):
        return (row_f == turned[0, pl.ds(r, 1), :]).astype(F32)

    counts = lax.fori_loop(
        0, CAP, lambda r, total: total + matches(r), jnp.zeros((DEV, 128), F32), unroll=8
    )
    most = jnp.max(jnp.sum(counts, axis=1, keepdims=True), axis=0, keepdims=True)
    before = jnp.dot(counts.astype(BF), ahead, preferred_element_type=F32)
    half_f = (row & (ON_CAP - 1)).astype(F32)
    upper = row < ON_CAP

    def rank(r, before):
        match = matches(r)
        ranking = jnp.sum(match * before, axis=0, keepdims=True)
        turned[1, pl.ds(r, 1), :] = ranking
        at = pl.ds(pl.multiple_of(r * 128, 128), 128)
        marks[:, at] = match.astype(BF)
        piece = jnp.where(upper, turned[2, pl.ds(r, 1), :], turned[3, pl.ds(r, 1), :])
        picks[:, at] = jnp.where(half_f == ranking, piece, 0.0).astype(BF)
        return before + match

    lax.fori_loop(0, CAP, rank, before, unroll=4)
    ranking = turned[1].T.astype(jnp.int32)
    second = (ranking >= ON_HALF).astype(jnp.int32)
    place = second * (ON_PACK - ON_HALF) + owners.astype(jnp.int32) * ON_STRIDE + ranking
    kept = jnp.logical_and(coded > 0, ranking < ON_CAP)
    onward_ref[...] = jnp.where(kept, place, 2 * ON_PACK)
    lists = lax.dot_general(
        picks[...], marks[...], (((1,), (1,)), ((), ())), preferred_element_type=F32
    ).T
    code_ref[...] = jnp.zeros((DEV, EXTRA, 128), F32)
    code_ref[:, 0, :] = lists
    code_ref[:, 1, :] = pltpu.roll(lists, ON_CAP, 1)
    most = most.astype(jnp.int32)
    code_ref[:, 2, :] = jnp.broadcast_to((most >> 6).astype(F32), (DEV, 128))
    code_ref[:, 3, :] = jnp.broadcast_to((most & 63).astype(F32), (DEV, 128))


def plan(received):
    square = jax.ShapeDtypeStruct((DEV, 128), jnp.int32)
    return pl.pallas_call(
        plan_kernel,
        in_specs=[pl.BlockSpec(memory_space=pltpu.VMEM)],
        out_specs=[pl.BlockSpec(memory_space=pltpu.VMEM)] * 3,
        out_shape=[square, square, jax.ShapeDtypeStruct((DEV, EXTRA, 128), F32)],
        scratch_shapes=[
            pltpu.VMEM((DEV * EXTRA, 128), F32),
            pltpu.VMEM((4, DEV, 128), F32),
            pltpu.VMEM((DEV, CAP * 128), BF),
            pltpu.VMEM((DEV, CAP * 128), BF),
        ],
        compiler_params=pltpu.CompilerParams(vmem_limit_bytes=VMEM),
        name="plan",
    )(received)


def fetch_kernel(slot_ref, done_ref, out_ref, source):
    low_row = low_lanes(1)

    def fetch(g, _):
        at = g * UN
        taken = []
        for u in range(UN):
            low = done_ref[pl.ds(slot_ref[at + u], 1), :]
            high = done_ref[pl.ds(slot_ref[at + u + PACK], 1), :]
            taken.append(jnp.where(low_row, low, high))
        for u in range(UN):
            source[pl.ds(at + u, 1), :] = taken[u]
        return 0

    lax.fori_loop(0, PACK // UN, fetch, 0)
    out_ref[...] = source[...].astype(BF)


def fetch_back(slots, done):
    return pl.pallas_call(
        fetch_kernel,
        in_specs=[
            pl.BlockSpec(memory_space=pltpu.SMEM),
            pl.BlockSpec(memory_space=pltpu.VMEM),
        ],
        out_specs=pl.BlockSpec(memory_space=pltpu.VMEM),
        out_shape=jax.ShapeDtypeStruct((PACK, 128), BF),
        scratch_shapes=[pltpu.VMEM((PACK, 128), F32)],
        compiler_params=pltpu.CompilerParams(vmem_limit_bytes=VMEM),
        name="fetch_back",
    )(slots, done)


def beside(sides, axis):
    forward = [(i, i + 1) for i in range(lax.axis_size(axis) - 1)]
    backward = [(target, source) for source, target in forward]
    return [
        lax.ppermute(sides[:, 1], axis, forward),
        lax.ppermute(sides[:, 0], axis, backward),
    ]


def ranks_of(owners):
    lanes = 128
    count = owners.shape[0]
    matches = (owners[None, :] == jnp.arange(DEV, dtype=jnp.int32)[:, None]).astype(BF)
    grouped = matches.reshape(DEV, count // lanes, lanes)
    index_row = jnp.arange(lanes, dtype=jnp.int32)
    strict = (index_row[:, None] < index_row[None, :]).astype(BF)
    within = jnp.einsum("dbi,ij->dbj", grouped, strict, preferred_element_type=F32)
    totals = jnp.sum(grouped.astype(F32), axis=2)
    before = jnp.cumsum(totals, axis=1) - totals
    ranking = jnp.sum(grouped.astype(F32) * (within + before[:, :, None]), axis=0)
    return ranking.reshape(count).astype(jnp.int32), matches, jnp.max(jnp.sum(totals, axis=1))


def place_of(owners, ranking, half, stride):
    return (ranking // half) * (DEV * stride) + owners * stride + ranking % half


def listed(matches, ranking, capacity, pieces):
    ranks = (ranking[:, None] == jnp.arange(capacity, dtype=jnp.int32)[None, :]).astype(BF)
    columns = jnp.concatenate([ranks * piece.astype(BF)[:, None] for piece in pieces], axis=1)
    return jnp.dot(matches, columns, preferred_element_type=F32).reshape(DEV, -1, capacity)


def code_rows(lists):
    _, count, capacity = lists.shape
    padded = jnp.pad(lists, ((0, 0), (0, EXTRA - count), (0, 128 - capacity)))
    return padded.reshape(DEV * EXTRA, 128)


def read_codes(packed, half, capacity, count):
    rows = packed.reshape(DEV, half + EXTRA, 128)
    return rows[:, half : half + count, :capacity].astype(jnp.int32)


def slot_pieces(slots):
    return [(slots + 1) // 64, (slots + 1) % 64]


def as_slots(high, low):
    coded = high * 64 + low
    return jnp.where(coded == 0, PTS, coded - 1)


def swap(values):
    return lax.all_to_all(values, ("gx", "gy"), split_axis=0, concat_axis=0, tiled=True)


def exchange(packed):
    rows = packed.shape[0]
    return swap(packed.reshape(DEV, rows // DEV, 128)).reshape(rows, 128)


def through_home(z_slots, z_dest, z_ranking, h_dest, done, weights):
    ranking, matches, _ = ranks_of(h_dest[0])
    h_lists = listed(matches, ranking, CAP, slot_pieces(h_dest[1]))
    h_lists = swap(h_lists.astype(jnp.int32).reshape(DEV, 2 * CAP))
    h_slots = as_slots(h_lists[:, :CAP], h_lists[:, CAP:]).reshape(-1)
    back_slots = z_slots.reshape(DEV, 2, HALF).transpose(1, 0, 2).reshape(-1)
    returned = exchange(fetch_back(back_slots, done))
    z_place = place_of(z_dest[0], z_ranking, HALF, HALF)
    h_place = place_of(h_dest[0], ranking, HALF, HALF)
    resent = relay(z_place, h_place, returned)
    return last_block(HALF, h_slots, exchange(resent), weights)


def local(
    feats,
    face_rows,
    neighbours,
    z_dest,
    h_dest,
    conv_weight,
    qkv_weight,
    out_weight,
    up_weight,
    down_weight,
    norm_gains,
):
    picked = jnp.take(feats, face_rows[0], axis=1)
    faces = beside(picked[:, 0:2], "gx") + beside(picked[:, 2:4], "gy")

    z_ranking, matches, _ = ranks_of(z_dest[0])
    z_place = place_of(z_dest[0], z_ranking, HALF, OUT_STRIDE)
    pieces = slot_pieces(z_dest[1]) + [h_dest[0], h_dest[1] // 64, h_dest[1] % 64]
    codes = code_rows(listed(matches, z_ranking, CAP, pieces))
    received = exchange(
        conv_send(neighbours, z_place, codes, feats, faces, conv_weight, norm_gains)
    )

    slots, onward, codes = plan(received)
    z_slots = slots[:, :CAP]
    codes = codes.reshape(DEV * EXTRA, 128)
    weights = (qkv_weight, out_weight, up_weight, down_weight, norm_gains.T)
    direct, done = first_block(slots.reshape(-1), onward.reshape(-1), received, codes, weights)
    direct = exchange(direct)
    codes = read_codes(direct, ON_HALF, ON_CAP, 4)
    direct_slots = as_slots(codes[:, 0], codes[:, 1]).reshape(-1)
    fits = jnp.max(codes[:, 2, 0] * 64 + codes[:, 3, 0]) <= ON_CAP
    return lax.cond(
        fits,
        lambda: last_block(ON_HALF, direct_slots, direct, weights),
        lambda: through_home(z_slots, z_dest, z_ranking, h_dest, done, weights),
    )


def solution(mesh):
    placed = (
        P(None, ("gx", "gy")),
        P(("gx", "gy"), None, None),
        P(None, ("gx", "gy")),
        P(None, ("gx", "gy")),
        P(None, ("gx", "gy")),
        P(),
        P(),
        P(),
        P(),
        P(),
        P(),
    )
    return jax.shard_map(
        local, mesh=mesh, in_specs=placed, out_specs=P(None, ("gx", "gy")), check_vma=False
    )
```

```python
import functools

import jax
import jax.numpy as jnp
from jax import lax
from jax.experimental import pallas as pl
from jax.experimental.pallas import tpu as pltpu
from jax.sharding import PartitionSpec as P

HEADS = 4
HEAD_DIM = 16
PATCH = 1024
C = 64
PTS = 4096
FACE = 128
EXT = PTS + 4 * FACE
TROWS = EXT + 8
DEV = 128
CAP = 48
HALF = CAP // 2
PACK = DEV * HALF
ON_CAP = 64
ON_HALF = ON_CAP // 2
EXTRA = 8
OUT_STRIDE = HALF + EXTRA
ON_STRIDE = ON_HALF + EXTRA
OUT_PACK = DEV * OUT_STRIDE
ON_PACK = DEV * ON_STRIDE
PAIRS = 13
BLK = 512
UN = 64
GROUP = 32
GROUPS = PTS // GROUP
LISTS = 4
LOG2_E = 1.4426950408889634
SAFE = 72.0
EPS = 1e-05
VMEM = 60 * 2**20
BF = jnp.bfloat16
F32 = jnp.float32


def lane_norm(values, gain):
    average = jnp.mean(values, axis=1, keepdims=True)
    centred = values - average
    spread = jnp.mean(centred * centred, axis=1, keepdims=True)
    return centred * lax.rsqrt(spread + EPS) * gain


def chan_norm(values, gain):
    average = jnp.mean(values, axis=0, keepdims=True)
    centred = values - average
    spread = jnp.mean(centred * centred, axis=0, keepdims=True)
    return centred * lax.rsqrt(spread + EPS) * gain


def low_lanes(rows):
    return lax.broadcasted_iota(jnp.int32, (rows, 128), 1) < C


def pack_rows(rows_ref, out_ref):
    count = out_ref.shape[0]

    def part(b, _):
        at = pl.multiple_of(b * 512, 512)
        low = rows_ref[pl.ds(at, 512), :]
        high = pltpu.roll(rows_ref[pl.ds(at + count, 512), :], C, 1)
        out_ref[pl.ds(at, 512), :] = jnp.where(low_lanes(512), low, high).astype(BF)
        return 0

    lax.fori_loop(0, count // 512, part, 0)


def unpack_rows(in_ref, rows_ref):
    count = in_ref.shape[0]

    def part(b, _):
        at = pl.multiple_of(b * 512, 512)
        both = in_ref[pl.ds(at, 512), :].astype(F32)
        rows_ref[pl.ds(at, 512), :] = both
        rows_ref[pl.ds(at + count, 512), :] = pltpu.roll(both, C, 1)
        return 0

    lax.fori_loop(0, count // 512, part, 0)


def move_rows(count, read, place_ref, rows_ref):
    def move(g, _):
        at = g * UN
        taken = [read(at + u) for u in range(UN)]
        for u in range(UN):
            rows_ref[pl.ds(place_ref[at + u], 1), :] = taken[u]
        return 0

    lax.fori_loop(0, count // UN, move, 0)


def put_codes(code_ref, rows_ref, half):
    def put(g, _):
        for u in range(8):
            d = g * 8 + u
            codes = code_ref[pl.ds(pl.multiple_of(d * EXTRA, EXTRA), EXTRA), :]
            at = pl.multiple_of(d * (half + EXTRA) + half, 8)
            rows_ref[pl.ds(at, EXTRA), :] = codes
        return 0

    lax.fori_loop(0, DEV // 8, put, 0)


def conv_kernel(
    near_ref, place_ref, code_ref, feats_ref, low_x, high_x, low_y, high_y, weight_ref, gain_ref,
    out_ref, *scratch,
):
    table, sums, rows, ext, orders = scratch[:5]
    lists, sems = scratch[5 : 5 + LISTS], scratch[5 + LISTS]

    def list_copy(g, b):
        return pltpu.make_async_copy(orders.at[g], lists[b], sems.at[b])

    offset = lax.broadcasted_iota(jnp.int32, (2 * PAIRS + 1, 128), 0)
    base = (offset - (offset > PAIRS).astype(jnp.int32)) // 2 * TROWS
    blank = jnp.zeros((32 - (2 * PAIRS + 1), 128), jnp.int32)
    for r in range(8):
        part = []
        for u in range(4 * r, 4 * r + 4):
            near = near_ref[:, u * 128 : (u + 1) * 128]
            part += [jnp.where(near < 0, EXT, near) + base, blank]
        orders[:, r, :] = jnp.concatenate(part, axis=0).T
    for b in range(LISTS):
        list_copy(b, b).start()

    def turn(b, _):
        at = pl.multiple_of(b * 512, 512)
        ext[pl.ds(at, 512), :] = feats_ref[:, pl.ds(at, 512)].astype(F32).T.astype(BF)
        return 0

    lax.fori_loop(0, PTS // 512, turn, 0)
    for i, face in enumerate((low_x, high_x, low_y, high_y)):
        ext[PTS + i * FACE : PTS + (i + 1) * FACE, :] = face[...].astype(F32).T.astype(BF)
    kept = [o for o in range(2 * PAIRS + 1) if o != PAIRS]
    pairs = [
        jnp.concatenate([weight_ref[kept[2 * j]], weight_ref[kept[2 * j + 1]]], axis=1)
        for j in range(PAIRS)
    ]

    def fill(b, _):
        at = pl.multiple_of(b * 512, 512)
        chunk = ext[pl.ds(at, 512), :]
        for j in range(PAIRS):
            table[pl.ds(pl.multiple_of(j * TROWS + at, 8), 512), :] = jnp.dot(
                chunk, pairs[j], preferred_element_type=F32
            )
        return 0

    lax.fori_loop(0, EXT // 512, fill, 0)
    for j in range(PAIRS):
        table[j * TROWS + EXT : (j + 1) * TROWS, :] = jnp.zeros((TROWS - EXT, 128), F32)

    low_row = low_lanes(1)

    def gather(step, _):
        for b in range(LISTS):
            g = step * LISTS + b
            list_copy(g, b).wait()
            for u in range(GROUP):
                even, odd = None, None
                for j in range(PAIRS):
                    at = u * 32 + kept[2 * j]
                    first = table[pl.ds(lists[b][at // 128, at % 128], 1), :]
                    at = u * 32 + kept[2 * j + 1]
                    second = table[pl.ds(lists[b][at // 128, at % 128], 1), :]
                    even = first if even is None else even + first
                    odd = second if odd is None else odd + second
                sums[pl.ds(u * GROUPS + g, 1), :] = jnp.where(low_row, even, odd)
            list_copy(jnp.minimum(g + LISTS, GROUPS - 1), b).start()
        return 0

    lax.fori_loop(0, GROUPS // LISTS, gather, 0)
    for b in range(LISTS):
        list_copy(GROUPS - 1, b).wait()

    def finish(b, _):
        at = pl.multiple_of(b * BLK, BLK)
        own = ext[pl.ds(at, BLK), :]
        both = sums[pl.ds(at, BLK), :]
        conv = both[:, :C] + both[:, C:] + jnp.dot(own, weight_ref[PAIRS], preferred_element_type=F32)
        sums[pl.ds(at, BLK), :C] = own.astype(F32) + lane_norm(conv, gain_ref[0:1, :])
        return 0

    lax.fori_loop(0, PTS // BLK, finish, 0)
    move_rows(PTS, lambda i: sums[pl.ds(i, 1), :], place_ref, rows)
    put_codes(code_ref, rows, HALF)
    pack_rows(rows, out_ref)


def conv_send(near, place, codes, feats, faces, weight, gains):
    return pl.pallas_call(
        conv_kernel,
        in_specs=[pl.BlockSpec(memory_space=pltpu.VMEM), pl.BlockSpec(memory_space=pltpu.SMEM)]
        + [pl.BlockSpec(memory_space=pltpu.VMEM)] * 8,
        out_specs=pl.BlockSpec(memory_space=pltpu.VMEM),
        out_shape=jax.ShapeDtypeStruct((OUT_PACK, 128), BF),
        scratch_shapes=[
            pltpu.VMEM((PAIRS * TROWS, 128), F32),
            pltpu.VMEM((PTS, 128), F32),
            pltpu.VMEM((2 * OUT_PACK, 128), F32),
            pltpu.VMEM((EXT, C), BF),
            pltpu.VMEM((GROUPS, 8, 128), jnp.int32),
        ]
        + [pltpu.SMEM((8, 128), jnp.int32)] * LISTS
        + [pltpu.SemaphoreType.DMA((LISTS,))],
        compiler_params=pltpu.CompilerParams(vmem_limit_bytes=VMEM),
        cost_estimate=pl.CostEstimate(flops=10**11, bytes_accessed=10**6, transcendentals=0),
        name="conv_send",
    )(near, place, codes, feats, *faces, weight, gains)


def relay_kernel(from_ref, to_ref, in_ref, out_ref, source, target):
    unpack_rows(in_ref, source)

    move_rows(PTS, lambda i: source[pl.ds(from_ref[i], 1), :], to_ref, target)
    pack_rows(target, out_ref)


def relay(place_from, place_to, packed):
    return pl.pallas_call(
        relay_kernel,
        in_specs=[
            pl.BlockSpec(memory_space=pltpu.SMEM),
            pl.BlockSpec(memory_space=pltpu.SMEM),
            pl.BlockSpec(memory_space=pltpu.VMEM),
        ],
        out_specs=pl.BlockSpec(memory_space=pltpu.VMEM),
        out_shape=jax.ShapeDtypeStruct((PACK, 128), BF),
        scratch_shapes=[
            pltpu.VMEM((2 * PACK, 128), F32),
            pltpu.VMEM((2 * PACK, 128), F32),
        ],
        compiler_params=pltpu.CompilerParams(vmem_limit_bytes=VMEM),
        cost_estimate=pl.CostEstimate(flops=10**9, bytes_accessed=10**6, transcendentals=0),
        name="relay",
    )(place_from, place_to, packed)


def turned_dot(weight, values):
    return lax.dot_general(
        weight, values, (((0,), (0,)), ((), ())), preferred_element_type=F32
    )


def patch_math(j, x, qkv_ref, outw_ref, up_ref, down_ref, gain_ref, mixed, values_ref):
    normed = chan_norm(x, gain_ref[:, 2 * j + 1 : 2 * j + 2]).astype(BF)
    qkv = turned_dot(qkv_ref[j], normed).astype(BF)
    queries = qkv[:C].astype(F32)
    keys = qkv[C : 2 * C].astype(F32)
    keys_t = keys.T
    head_of = lax.broadcasted_iota(jnp.int32, (C, PATCH), 0) // HEAD_DIM
    ones = jnp.ones((HEAD_DIM, PATCH), BF)

    def of_head(h, values):
        return jnp.where(head_of == h, values, 0.0)

    def weighted(values, weights):
        summed = jnp.dot(
            jnp.concatenate([values, ones], axis=0), weights, preferred_element_type=F32
        )
        return (summed[:HEAD_DIM] / summed[HEAD_DIM : HEAD_DIM + 1]).astype(BF)

    def longest(values):
        squares = (values * values).reshape(HEADS, HEAD_DIM, PATCH)
        return jnp.max(jnp.sum(squares, axis=1), axis=1, keepdims=True)

    reach = jnp.max(longest(queries) * longest(keys))
    safe = reach <= (SAFE * HEAD_DIM**0.5) ** 2

    @pl.when(safe)
    def _():
        scaled = queries * (HEAD_DIM**-0.5 * LOG2_E)
        upper = scaled.astype(BF).astype(F32)
        lower = scaled - upper
        keys_2 = jnp.concatenate([keys_t, keys_t], axis=1).astype(BF)
        for h in range(HEADS):
            split = jnp.concatenate([of_head(h, upper), of_head(h, lower)], axis=0).astype(BF)
            scores = jnp.dot(keys_2, split, preferred_element_type=F32)
            first = h * HEAD_DIM
            values = qkv[2 * C + first : 2 * C + first + HEAD_DIM]
            mixed[first : first + HEAD_DIM, :] = weighted(values, jnp.exp2(scores).astype(BF))

    @pl.when(jnp.logical_not(safe))
    def _():
        keys_1 = keys_t.astype(BF)
        values_ref[...] = qkv[2 * C :]

        def head(h, _):
            one_head = of_head(h, queries * HEAD_DIM**-0.5).astype(BF)
            scores = jnp.dot(keys_1, one_head, preferred_element_type=F32)
            weights = jnp.exp(scores - jnp.max(scores, axis=0, keepdims=True)).astype(BF)
            at = pl.ds(pl.multiple_of(h * HEAD_DIM, HEAD_DIM), HEAD_DIM)
            mixed[at, :] = weighted(values_ref[at, :], weights)
            return 0

        lax.fori_loop(0, HEADS, head, 0)

    residual = x + turned_dot(outw_ref[j], mixed[...])
    normed_b = chan_norm(residual, gain_ref[:, 2 * j + 2 : 2 * j + 3]).astype(BF)
    raised = turned_dot(up_ref[j], normed_b)
    hidden = (0.5 * raised * (1.0 + lax.erf(raised * 0.5**0.5))).astype(BF)
    return residual + turned_dot(down_ref[j], hidden)


def place_rows(half, span, slot_ref, in_ref, source, rows):
    unpack_rows(in_ref, source)
    count = in_ref.shape[0]
    stride = count // DEV

    first = CAP // 3 if 2 * half == CAP else CAP

    def place(d, _):
        def some(ranks):
            taken = [
                source[pl.ds(k // half * count + d * stride + k % half, 1), :] for k in ranks
            ]
            for k, value in zip(ranks, taken):
                rows[pl.ds(slot_ref[d * span + k], 1), :] = value

        some(range(first))

        @pl.when(slot_ref[d * span + first] < PTS)
        def _():
            some(range(first, 2 * half))

        return 0

    lax.fori_loop(0, DEV, place, 0)


def first_kernel(
    slot_ref, onward_ref, in_ref, code_ref, qkv_ref, outw_ref, up_ref, down_ref, gain_ref,
    out_ref, done_ref, source, rows, mixed, values_ref,
):
    place_rows(HALF, 128, slot_ref, in_ref, source, rows)
    done_ref[PTS:, :] = jnp.zeros((8, 128), F32)

    def patch(p, _):
        at = pl.multiple_of(p * PATCH, PATCH)
        x = rows[pl.ds(at, PATCH), :].T[:C]
        y = patch_math(0, x, qkv_ref, outw_ref, up_ref, down_ref, gain_ref, mixed, values_ref)
        y = y.astype(BF).astype(F32)
        done_ref[pl.ds(at, PATCH), :] = jnp.concatenate([y, y], axis=0).T
        return 0

    lax.fori_loop(0, PTS // PATCH, patch, 0)

    def send(d, _):
        def some(ranks):
            taken = [done_ref[pl.ds(slot_ref[d * 128 + k], 1), :] for k in ranks]
            for k, value in zip(ranks, taken):
                source[pl.ds(onward_ref[d * 128 + k], 1), :] = value

        some(range(CAP // 3))

        @pl.when(slot_ref[d * 128 + CAP // 3] < PTS)
        def _():
            some(range(CAP // 3, CAP))

        return 0

    lax.fori_loop(0, DEV, send, 0)
    put_codes(code_ref, source, ON_HALF)
    pack_rows(source, out_ref)


def last_kernel(
    half, slot_ref, in_ref, qkv_ref, outw_ref, up_ref, down_ref, gain_ref,
    out_ref, source, rows, mixed, values_ref,
):
    place_rows(half, 2 * half, slot_ref, in_ref, source, rows)

    def patch(p, _):
        at = pl.multiple_of(p * PATCH, PATCH)
        x = rows[pl.ds(at, PATCH), :].T[:C]
        y = patch_math(1, x, qkv_ref, outw_ref, up_ref, down_ref, gain_ref, mixed, values_ref)
        out_ref[:, pl.ds(at, PATCH)] = y.astype(BF)
        return 0

    lax.fori_loop(0, PTS // PATCH, patch, 0)


def block_call(kernel, lists, operands, out_shape, buffer_rows, name):
    return pl.pallas_call(
        kernel,
        in_specs=[pl.BlockSpec(memory_space=pltpu.SMEM)] * len(lists)
        + [pl.BlockSpec(memory_space=pltpu.VMEM)] * len(operands),
        out_specs=jax.tree.map(lambda _: pl.BlockSpec(memory_space=pltpu.VMEM), out_shape),
        out_shape=out_shape,
        scratch_shapes=[
            pltpu.VMEM((buffer_rows, 128), F32),
            pltpu.VMEM((PTS + 8, 128), F32),
            pltpu.VMEM((C, PATCH), BF),
            pltpu.VMEM((C, PATCH), BF),
        ],
        compiler_params=pltpu.CompilerParams(vmem_limit_bytes=VMEM),
        cost_estimate=pl.CostEstimate(flops=4 * 10**10, bytes_accessed=10**6, transcendentals=0),
        name=name,
    )(*lists, *operands)


def first_block(slots, onward, packed, codes, weights):
    shapes = (
        jax.ShapeDtypeStruct((ON_PACK, 128), BF),
        jax.ShapeDtypeStruct((PTS + 8, 128), F32),
    )
    return block_call(
        first_kernel, (slots, onward), (packed, codes, *weights), shapes, 2 * ON_PACK + 8,
        "first_block",
    )


def last_block(half, slots, packed, weights):
    return block_call(
        functools.partial(last_kernel, half), (slots,), (packed, *weights),
        jax.ShapeDtypeStruct((C, PTS), BF), 2 * packed.shape[0], "last_block",
    )


def plan_kernel(in_ref, slot_ref, onward_ref, code_ref, mine, turned, marks, picks):
    def take(d, _):
        tile = in_ref[pl.ds(pl.multiple_of(d * OUT_STRIDE + HALF - EXTRA, 16), 16), :]
        mine[pl.ds(pl.multiple_of(d * EXTRA, EXTRA), EXTRA), :] = tile.astype(F32)[EXTRA:]
        return 0

    lax.fori_loop(0, DEV, take, 0, unroll=8)
    high, low, owner, next_high, next_low = (
        mine[pl.ds(p, DEV, stride=EXTRA), :] for p in range(5)
    )
    coded = (high * 64.0 + low).astype(jnp.int32)
    slot_ref[...] = jnp.where(coded == 0, PTS, coded - 1)
    owners = jnp.where(coded == 0, float(DEV), owner)
    following = (next_high * 64.0 + next_low).astype(jnp.int32) + 1
    turned[0] = owners.T
    turned[1] = jnp.zeros((DEV, 128), F32)
    turned[2] = (following >> 6).astype(F32).T
    turned[3] = (following & 63).astype(F32).T
    row = lax.broadcasted_iota(jnp.int32, (DEV, 128), 0)
    row_f = row.astype(F32)
    ahead = (row < lax.broadcasted_iota(jnp.int32, (DEV, 128), 1)).astype(F32).astype(BF)

    def matches(r):
        return (row_f == turned[0, pl.ds(r, 1), :]).astype(F32)

    counts = lax.fori_loop(
        0, CAP, lambda r, total: total + matches(r), jnp.zeros((DEV, 128), F32), unroll=8
    )
    most = jnp.max(jnp.sum(counts, axis=1, keepdims=True), axis=0, keepdims=True)
    before = jnp.dot(counts.astype(BF), ahead, preferred_element_type=F32)
    half_f = (row & (ON_CAP - 1)).astype(F32)
    upper = row < ON_CAP

    def rank(r, before):
        match = matches(r)
        ranking = jnp.sum(match * before, axis=0, keepdims=True)
        turned[1, pl.ds(r, 1), :] = ranking
        at = pl.ds(pl.multiple_of(r * 128, 128), 128)
        marks[:, at] = match.astype(BF)
        piece = jnp.where(upper, turned[2, pl.ds(r, 1), :], turned[3, pl.ds(r, 1), :])
        picks[:, at] = jnp.where(half_f == ranking, piece, 0.0).astype(BF)
        return before + match

    lax.fori_loop(0, CAP, rank, before, unroll=4)
    ranking = turned[1].T.astype(jnp.int32)
    second = (ranking >= ON_HALF).astype(jnp.int32)
    place = second * (ON_PACK - ON_HALF) + owners.astype(jnp.int32) * ON_STRIDE + ranking
    kept = jnp.logical_and(coded > 0, ranking < ON_CAP)
    onward_ref[...] = jnp.where(kept, place, 2 * ON_PACK)
    lists = lax.dot_general(
        picks[...], marks[...], (((1,), (1,)), ((), ())), preferred_element_type=F32
    ).T
    code_ref[...] = jnp.zeros((DEV, EXTRA, 128), F32)
    code_ref[:, 0, :] = lists
    code_ref[:, 1, :] = pltpu.roll(lists, ON_CAP, 1)
    most = most.astype(jnp.int32)
    code_ref[:, 2, :] = jnp.broadcast_to((most >> 6).astype(F32), (DEV, 128))
    code_ref[:, 3, :] = jnp.broadcast_to((most & 63).astype(F32), (DEV, 128))


def plan(received):
    square = jax.ShapeDtypeStruct((DEV, 128), jnp.int32)
    return pl.pallas_call(
        plan_kernel,
        in_specs=[pl.BlockSpec(memory_space=pltpu.VMEM)],
        out_specs=[pl.BlockSpec(memory_space=pltpu.VMEM)] * 3,
        out_shape=[square, square, jax.ShapeDtypeStruct((DEV, EXTRA, 128), F32)],
        scratch_shapes=[
            pltpu.VMEM((DEV * EXTRA, 128), F32),
            pltpu.VMEM((4, DEV, 128), F32),
            pltpu.VMEM((DEV, CAP * 128), BF),
            pltpu.VMEM((DEV, CAP * 128), BF),
        ],
        compiler_params=pltpu.CompilerParams(vmem_limit_bytes=VMEM),
        name="plan",
    )(received)


def fetch_kernel(slot_ref, done_ref, out_ref, source):
    low_row = low_lanes(1)

    def fetch(g, _):
        at = g * UN
        taken = []
        for u in range(UN):
            low = done_ref[pl.ds(slot_ref[at + u], 1), :]
            high = done_ref[pl.ds(slot_ref[at + u + PACK], 1), :]
            taken.append(jnp.where(low_row, low, high))
        for u in range(UN):
            source[pl.ds(at + u, 1), :] = taken[u]
        return 0

    lax.fori_loop(0, PACK // UN, fetch, 0)
    out_ref[...] = source[...].astype(BF)


def fetch_back(slots, done):
    return pl.pallas_call(
        fetch_kernel,
        in_specs=[
            pl.BlockSpec(memory_space=pltpu.SMEM),
            pl.BlockSpec(memory_space=pltpu.VMEM),
        ],
        out_specs=pl.BlockSpec(memory_space=pltpu.VMEM),
        out_shape=jax.ShapeDtypeStruct((PACK, 128), BF),
        scratch_shapes=[pltpu.VMEM((PACK, 128), F32)],
        compiler_params=pltpu.CompilerParams(vmem_limit_bytes=VMEM),
        name="fetch_back",
    )(slots, done)


def beside(sides, axis):
    forward = [(i, i + 1) for i in range(lax.axis_size(axis) - 1)]
    backward = [(target, source) for source, target in forward]
    return [
        lax.ppermute(sides[:, 1], axis, forward),
        lax.ppermute(sides[:, 0], axis, backward),
    ]


def ranks_of(owners):
    lanes = 128
    count = owners.shape[0]
    matches = (owners[None, :] == jnp.arange(DEV, dtype=jnp.int32)[:, None]).astype(BF)
    grouped = matches.reshape(DEV, count // lanes, lanes)
    index_row = jnp.arange(lanes, dtype=jnp.int32)
    strict = (index_row[:, None] < index_row[None, :]).astype(BF)
    within = jnp.einsum("dbi,ij->dbj", grouped, strict, preferred_element_type=F32)
    totals = jnp.sum(grouped.astype(F32), axis=2)
    before = jnp.cumsum(totals, axis=1) - totals
    ranking = jnp.sum(grouped.astype(F32) * (within + before[:, :, None]), axis=0)
    return ranking.reshape(count).astype(jnp.int32), matches, jnp.max(jnp.sum(totals, axis=1))


def place_of(owners, ranking, half, stride):
    return (ranking // half) * (DEV * stride) + owners * stride + ranking % half


def listed(matches, ranking, capacity, pieces):
    ranks = (ranking[:, None] == jnp.arange(capacity, dtype=jnp.int32)[None, :]).astype(BF)
    columns = jnp.concatenate([ranks * piece.astype(BF)[:, None] for piece in pieces], axis=1)
    return jnp.dot(matches, columns, preferred_element_type=F32).reshape(DEV, -1, capacity)


def code_rows(lists):
    _, count, capacity = lists.shape
    padded = jnp.pad(lists, ((0, 0), (0, EXTRA - count), (0, 128 - capacity)))
    return padded.reshape(DEV * EXTRA, 128)


def read_codes(packed, half, capacity, count):
    rows = packed.reshape(DEV, half + EXTRA, 128)
    return rows[:, half : half + count, :capacity].astype(jnp.int32)


def slot_pieces(slots):
    return [(slots + 1) // 64, (slots + 1) % 64]


def as_slots(high, low):
    coded = high * 64 + low
    return jnp.where(coded == 0, PTS, coded - 1)


def swap(values):
    return lax.all_to_all(values, ("gx", "gy"), split_axis=0, concat_axis=0, tiled=True)


def exchange(packed):
    rows = packed.shape[0]
    return swap(packed.reshape(DEV, rows // DEV, 128)).reshape(rows, 128)


def through_home(z_slots, z_dest, z_ranking, h_dest, done, weights):
    ranking, matches, _ = ranks_of(h_dest[0])
    h_lists = listed(matches, ranking, CAP, slot_pieces(h_dest[1]))
    h_lists = swap(h_lists.astype(jnp.int32).reshape(DEV, 2 * CAP))
    h_slots = as_slots(h_lists[:, :CAP], h_lists[:, CAP:]).reshape(-1)
    back_slots = z_slots.reshape(DEV, 2, HALF).transpose(1, 0, 2).reshape(-1)
    returned = exchange(fetch_back(back_slots, done))
    z_place = place_of(z_dest[0], z_ranking, HALF, HALF)
    h_place = place_of(h_dest[0], ranking, HALF, HALF)
    resent = relay(z_place, h_place, returned)
    return last_block(HALF, h_slots, exchange(resent), weights)


def local(
    feats,
    face_rows,
    neighbours,
    z_dest,
    h_dest,
    conv_weight,
    qkv_weight,
    out_weight,
    up_weight,
    down_weight,
    norm_gains,
):
    picked = jnp.take(feats, face_rows[0], axis=1)
    faces = beside(picked[:, 0:2], "gx") + beside(picked[:, 2:4], "gy")

    z_ranking, matches, _ = ranks_of(z_dest[0])
    z_place = place_of(z_dest[0], z_ranking, HALF, OUT_STRIDE)
    pieces = slot_pieces(z_dest[1]) + [h_dest[0], h_dest[1] // 64, h_dest[1] % 64]
    codes = code_rows(listed(matches, z_ranking, CAP, pieces))
    received = exchange(
        conv_send(neighbours, z_place, codes, feats, faces, conv_weight, norm_gains)
    )

    slots, onward, codes = plan(received)
    z_slots = slots[:, :CAP]
    codes = codes.reshape(DEV * EXTRA, 128)
    weights = (qkv_weight, out_weight, up_weight, down_weight, norm_gains.T)
    direct, done = first_block(slots.reshape(-1), onward.reshape(-1), received, codes, weights)
    direct = exchange(direct)
    codes = read_codes(direct, ON_HALF, ON_CAP, 4)
    direct_slots = as_slots(codes[:, 0], codes[:, 1]).reshape(-1)
    fits = jnp.max(codes[:, 2, 0] * 64 + codes[:, 3, 0]) <= ON_CAP
    return lax.cond(
        fits,
        lambda: last_block(ON_HALF, direct_slots, direct, weights),
        lambda: through_home(z_slots, z_dest, z_ranking, h_dest, done, weights),
    )


def solution(mesh):
    placed = (
        P(None, ("gx", "gy")),
        P(("gx", "gy"), None, None),
        P(None, ("gx", "gy")),
        P(None, ("gx", "gy")),
        P(None, ("gx", "gy")),
        P(),
        P(),
        P(),
        P(),
        P(),
        P(),
    )
    return jax.shard_map(
        local, mesh=mesh, in_specs=placed, out_specs=P(None, ("gx", "gy")), check_vma=False
    )
```
